512 devices in a mesh: chan: 16 (over y_hi, x), tm: 32 (over y_lo, z, core).
Axes of the slice: x: 4, y: 8 (y_hi: 4, y_lo: 2; y = y_hi * 2 + y_lo), z: 8, core: 2. Of those that a mesh axis runs over, the one named last changes fastest.
Arguments:
- record: bfloat16 [2048, 65536], P('chan', 'tm')
- blocks: int32 [4], replicated, may hold values from 0 to 127
- offsets: int32 [64], P('tm'), may hold values from -16 to 16, as said below
Outputs:
- stack: float32 [64, 33, 2048], P('tm', None, 'chan')
The draws below stay inside these ranges and needn't reach their ends.
Inputs may be any that keep to these rules, and one draw needn't show every extreme that they name: both -16 and 16 occur among the offsets.
All inputs are finite; a program needn't handle non-finite values. Where the reference program divides by a largest or mean magnitude, that divisor is 1e-20 or more.
Results may differ from the reference program's by a relative error of at most 0.0003.
Values may be sent and summed in bfloat16 or wider, within the bound.
A program may use at most 64 MiB of HBM per device.

```python
import math
import jax
import jax.numpy as jnp
from jax import lax

SAMPLES = 1024
LAG = 16
BLOCK = 16
NBLK = 4
LAGS = 33
SOURCES = 64
CHANNELS = 2048
WINDOWS = 64


def draw_record(key, part):
    key = jax.random.fold_in(key, 7)
    first_key = jax.random.fold_in(key, 0)
    second_key = jax.random.fold_in(key, 1)
    fourth_key = jax.random.fold_in(key, 3)
    fifth_key = jax.random.fold_in(key, 4)
    length = WINDOWS * SAMPLES
    scales = jnp.exp(jax.random.uniform(second_key, (CHANNELS, WINDOWS, 1), jnp.float32, 0.0, math.log(10.0)))
    delays = jax.random.randint(fourth_key, (CHANNELS, 1), 0, LAG + 1, jnp.int32)
    noise = jax.random.normal(first_key, (CHANNELS, length), jnp.float32)
    wave = jax.random.normal(fifth_key, (length + LAG,), jnp.float32)
    arrived = jnp.zeros((CHANNELS, length), jnp.float32)
    for shift in range(LAG + 1):
        moved = wave[LAG - shift:LAG - shift + length][None, :]
        arrived = arrived + jnp.where(delays == shift, moved, 0.0)
    total = (noise + arrived).reshape(CHANNELS, WINDOWS, SAMPLES) * scales
    return total.reshape(CHANNELS, length).astype(jnp.bfloat16)


def draw_offsets(key, part):
    key = jax.random.fold_in(key, 5)
    first_key, second_key = jax.random.split(key)
    shifts = jax.random.randint(first_key, (WINDOWS,), -LAG, LAG + 1, jnp.int32)
    order = jax.random.permutation(second_key, WINDOWS)
    shifts = shifts.at[order[0]].set(-LAG)
    return shifts.at[order[1]].set(LAG)


def place_ends(entries, key, smallest, top_value):
    spot = [jax.random.randint(jax.random.fold_in(key, axis), (), 0, length) for axis, length in enumerate(entries.shape)]
    widest = entries.shape.index(max(entries.shape))
    next_to = spot[:widest] + [(spot[widest] + 1) % entries.shape[widest]] + spot[widest + 1:]
    return entries.at[tuple(spot)].set(smallest).at[tuple(next_to)].set(top_value)


def setup_inputs(seed: int = 0) -> dict:
    arg_keys = jax.random.split(jax.random.key(seed), 4)
    record = draw_record(jax.random.fold_in(arg_keys[3], 71), 0)
    blocks = place_ends(jax.random.randint(arg_keys[1], (NBLK,), 0, CHANNELS // BLOCK), jax.random.fold_in(arg_keys[1], 1), 0, (CHANNELS // BLOCK) - 1).astype(jnp.int32)
    offsets = draw_offsets(jax.random.fold_in(arg_keys[3], 71), 0)
    return dict(record=record, blocks=blocks, offsets=offsets)


epsilon = 1e-6


def shifted_copies(segment, reach):
    length = segment.shape[1]
    padded = jnp.pad(segment, ((0, 0), (2 * reach, 2 * reach)))
    copies = [padded[:, reach - lag_value: reach - lag_value + length + 2 * reach] for lag_value in range(-reach, reach + 1)]
    return jnp.stack(copies, axis=1).reshape(segment.shape[0] * (2 * reach + 1), length + 2 * reach)


def reference(record, blocks, offsets):
    values = record.astype(jnp.float32).reshape(CHANNELS, WINDOWS, SAMPLES)
    magnitude = jnp.mean(jnp.abs(values), axis=2, keepdims=True)
    normed = (values / (magnitude + epsilon)).reshape(CHANNELS, WINDOWS * SAMPLES).astype(jnp.bfloat16)
    padded = jnp.pad(normed, ((0, 0), (2 * LAG, 2 * LAG)))
    full_width = padded.shape[1]
    pieces = []
    for block_pos in range(NBLK):
        first_channel = (blocks[block_pos] * BLOCK).astype(jnp.int32)
        pieces.append(lax.dynamic_slice(padded, (first_channel, jnp.int32(0)), (BLOCK, full_width)))
    sources = jnp.concatenate(pieces, axis=0)

    def one_window(window, total):
        window = jnp.asarray(window).astype(jnp.int32)
        begin_at = (window * SAMPLES + offsets[window]).astype(jnp.int32)
        receivers = lax.dynamic_slice(padded, (jnp.int32(0), begin_at + LAG), (CHANNELS, SAMPLES + 2 * LAG))
        segment = lax.dynamic_slice(sources, (jnp.int32(0), begin_at + 2 * LAG), (SOURCES, SAMPLES))
        product = lax.dot_general(shifted_copies(segment, LAG), receivers, (((1,), (1,)), ((), ())), preferred_element_type=jnp.float32)
        return total + product

    total = lax.fori_loop(0, WINDOWS, one_window, jnp.zeros((SOURCES * LAGS, CHANNELS), jnp.float32))
    scale = 1.0 / (float(WINDOWS * SAMPLES) ** 0.5)
    return total.reshape(SOURCES, LAGS, CHANNELS) * scale
```

```python
import functools
import math

import jax
import jax.numpy as jnp
from jax import lax
from jax.experimental import pallas as pl
from jax.experimental.pallas import tpu as pltpu
from jax.sharding import PartitionSpec as P

LAG = 16
BLOCK = 16
NBLK = 4
LAGS = 33
EPS = 1e-06
LANE = 128
SHIFTS = LAG + 1
ROWS = 72
MESH = pl.DeviceIdType.MESH


def shifted(before, here, count):
    if count == 0:
        return here
    lane = lax.broadcasted_iota(jnp.int32, here.shape, here.ndim - 1)
    axis = here.ndim - 1
    return jnp.where(lane < count, pltpu.roll(before, count, axis), pltpu.roll(here, count, axis))


def kernel(
    n_chan, n_tm, blocks_ref, offsets_ref, record_ref, out_ref,
    raw, normed, halo_left, halo_right, edge_out, edge_left, edge_right,
    cand, p1, srcs, both, lhs, low, high, psend, crecv, mine, p3,
    in_sem, halo_send, halo_recv, p1_send, p1_recv, p2_send, p2_recv,
    core_send, core_recv, p3_send, p3_recv,
):
    chan = lax.axis_index("chan")
    tm = lax.axis_index("tm")
    chips = n_tm // 2
    core = lax.rem(tm, 2)
    chip = lax.div(tm, 2)
    right = lax.rem(tm + 1, n_tm)
    left = lax.rem(tm + n_tm - 1, n_tm)
    n_chunk = normed.shape[2] // LANE
    samples = normed.shape[2] // 2

    load = pltpu.make_async_copy(record_ref, raw, in_sem)
    load.start()

    barrier = pltpu.get_barrier_semaphore()
    for j in range(1, n_chan):
        pl.semaphore_signal(barrier, inc=1, device_id=(lax.rem(chan + j, n_chan), tm), device_id_type=MESH)
    for j in range(1, chips):
        pl.semaphore_signal(
            barrier, inc=1, device_id=(chan, lax.rem(chip + j, chips) * 2 + core), device_id_type=MESH
        )
    pl.semaphore_signal(barrier, inc=1, device_id=(chan, left), device_id_type=MESH)
    pl.semaphore_signal(barrier, inc=1, device_id=(chan, right), device_id_type=MESH)

    load.wait()
    for row in range(raw.shape[0]):
        for window in range(2):
            cols = pl.ds(window * samples, samples)
            values = raw[row, :, cols].astype(jnp.float32)
            magnitude = jnp.mean(jnp.abs(values), axis=1, keepdims=True)
            normed[row, :, cols] = (values / (magnitude + EPS)).astype(jnp.bfloat16)

    for k in range(NBLK):
        rows = normed[lax.rem(blocks_ref[k], raw.shape[0])]
        for j in range(n_chunk):
            cand[j, k] = rows[:, j * LANE : (j + 1) * LANE]
    edge_out[0] = jnp.full((16, LANE), offsets_ref[0], jnp.int32).astype(jnp.float32).astype(jnp.bfloat16)
    edge_out[1] = jnp.full((16, LANE), offsets_ref[1], jnp.int32).astype(jnp.float32).astype(jnp.bfloat16)

    pl.semaphore_wait(barrier, n_chan + chips)

    p1_copies = []
    for j in range(1, n_chan):
        peer = lax.rem(chan + j, n_chan)
        copy = pltpu.make_async_remote_copy(
            src_ref=cand.at[peer], dst_ref=p1.at[chan], send_sem=p1_send, recv_sem=p1_recv,
            device_id=(peer, tm), device_id_type=MESH,
        )
        copy.start()
        p1_copies.append(copy)
    own = pltpu.make_async_copy(cand.at[chan], p1.at[chan], p1_recv)
    own.start()
    halo_copies = [
        pltpu.make_async_remote_copy(
            src_ref=normed.at[:, :, pl.ds((n_chunk - 1) * LANE, LANE)], dst_ref=halo_left,
            send_sem=halo_send.at[0], recv_sem=halo_recv.at[0], device_id=(chan, right), device_id_type=MESH,
        ),
        pltpu.make_async_remote_copy(
            src_ref=normed.at[:, :, pl.ds(0, LANE)], dst_ref=halo_right,
            send_sem=halo_send.at[1], recv_sem=halo_recv.at[1], device_id=(chan, left), device_id_type=MESH,
        ),
        pltpu.make_async_remote_copy(
            src_ref=edge_out.at[1], dst_ref=edge_left,
            send_sem=halo_send.at[2], recv_sem=halo_recv.at[2], device_id=(chan, right), device_id_type=MESH,
        ),
        pltpu.make_async_remote_copy(
            src_ref=edge_out.at[0], dst_ref=edge_right,
            send_sem=halo_send.at[3], recv_sem=halo_recv.at[3], device_id=(chan, left), device_id_type=MESH,
        ),
    ]
    for copy in halo_copies:
        copy.start()
    for copy in halo_copies:
        copy.wait()

    at_start = tm == 0
    at_end = tm == n_tm - 1
    zero = jnp.zeros((16, LANE), jnp.bfloat16)
    for row in range(raw.shape[0]):
        before = jnp.where(at_start, zero, halo_left[row])
        after = jnp.where(at_end, zero, halo_right[row])
        for b in range(n_chunk + 1):
            here = normed[row, :, b * LANE : (b + 1) * LANE] if b < n_chunk else after
            both[row * 16 : row * 16 + 16, b * LANE : (b + 1) * LANE] = shifted(before, here, LAG)
            both[LANE + row * 16 : LANE + row * 16 + 16, b * LANE : (b + 1) * LANE] = here
            before = here

    at = lax.broadcasted_iota(jnp.int32, (16, LANE), 1) + chan * LANE
    count = ((at >= offsets_ref[0]) & (at < samples + offsets_ref[0])).astype(jnp.float32)
    count += ((at >= samples + offsets_ref[1]) & (at < 2 * samples + offsets_ref[1])).astype(jnp.float32)
    at_f = at.astype(jnp.float32)
    covered = (at_f < edge_left[...].astype(jnp.float32)).astype(jnp.float32)
    count += jnp.where(at_start, jnp.zeros_like(covered), covered)
    covered = (at_f >= 2.0 * samples + edge_right[...].astype(jnp.float32)).astype(jnp.float32)
    count += jnp.where(at_end, jnp.zeros_like(covered), covered)

    pltpu.make_async_copy(p1, p1, p1_recv).wait()
    for k in range(NBLK):
        piece = p1[lax.div(blocks_ref[k], raw.shape[0]), k].astype(jnp.float32)
        srcs[chan, k] = (piece * count).astype(jnp.bfloat16)

    for j in range(1, n_chan):
        peer = lax.rem(chan + j, n_chan)
        pltpu.make_async_remote_copy(
            src_ref=srcs.at[chan], dst_ref=srcs.at[chan], send_sem=p2_send, recv_sem=p2_recv,
            device_id=(peer, tm), device_id_type=MESH,
        ).start()
    for copy in p1_copies:
        copy.wait_send()
    others = srcs.at[pl.ds(0, n_chan - 1)]
    pltpu.make_async_copy(others, others, p2_recv).wait()

    core_copies = []
    for k in range(NBLK):
        for i in range(SHIFTS):
            before = zero
            for b in range(n_chunk + 1):
                here = srcs[b, k] if b < n_chunk else zero
                lhs[i * 16 : i * 16 + 16, b * LANE : (b + 1) * LANE] = shifted(before, here, i)
                before = here
        found = lax.dot_general(
            lhs[...], both[...], (((1,), (1,)), ((), ())), preferred_element_type=jnp.float32
        ) * (1.0 / math.sqrt(n_tm * 2 * samples))
        low[...] = found[:, :LANE]
        high[...] = found[:, LANE:]
        for s in range(BLOCK):
            pair = s // 2
            c, to, at_row = pair % 2, k * 4 + pair // 2, (s % 2) * 32
            psend[c, to, at_row : at_row + 16] = low[pl.ds(s, 16, stride=16), :]
            psend[c, to, at_row + 16 : at_row + 32] = high[pl.ds(s, 16, stride=16), :]
        for pair in range(BLOCK // 2):
            c, to = pair % 2, k * 4 + pair // 2
            psend[c, to, 64:66] = high[256 + 2 * pair : 258 + 2 * pair, :]
        copy = pltpu.make_async_remote_copy(
            src_ref=psend.at[1 - core, pl.ds(4 * k, 4)], dst_ref=crecv.at[pl.ds(4 * k, 4)],
            send_sem=core_send.at[k], recv_sem=core_recv.at[k], device_id=(chan, tm + 1 - 2 * core), device_id_type=MESH,
        )
        copy.start()
        core_copies.append(copy)

    for k in range(NBLK):
        core_copies[k].wait_recv()
        for q in range(4):
            mine[4 * k + q] = psend[core, 4 * k + q] + crecv[4 * k + q]
    for j in range(1, chips):
        peer = lax.rem(chip + j, chips)
        pltpu.make_async_remote_copy(
            src_ref=mine.at[peer], dst_ref=p3.at[chip], send_sem=p3_send, recv_sem=p3_recv,
            device_id=(chan, peer * 2 + core), device_id_type=MESH,
        ).start()
    own = pltpu.make_async_copy(mine.at[chip], p3.at[chip], p3_recv)
    own.start()
    pltpu.make_async_copy(p3, p3, p3_recv).wait()
    total = p3[0]
    for j in range(1, chips):
        total = total + p3[j]
    out_ref[0, 0:32] = total[0:32]
    out_ref[1, 0:32] = total[32:64]
    out_ref[0, 32:33] = total[64:65]
    out_ref[1, 32:33] = total[65:66]

    pltpu.make_async_copy(others, others, p2_send).wait()
    for copy in core_copies:
        copy.wait_send()
    sent = p3.at[pl.ds(0, chips - 1)]
    pltpu.make_async_copy(sent, sent, p3_send).wait()


def local(n_chan, n_tm, record, blocks, offsets):
    channels, width = record.shape
    groups = channels // BLOCK
    n_chunk = width // LANE
    chips = n_tm // 2
    bf16, f32 = jnp.bfloat16, jnp.float32
    dma = pltpu.SemaphoreType.DMA
    wide = (n_chunk + 1) * LANE
    return pl.pallas_call(
        functools.partial(kernel, n_chan, n_tm),
        out_shape=jax.ShapeDtypeStruct((2, LAGS, channels), f32),
        in_specs=[
            pl.BlockSpec(memory_space=pltpu.SMEM),
            pl.BlockSpec(memory_space=pltpu.SMEM),
            pl.BlockSpec(memory_space=pl.ANY),
        ],
        out_specs=pl.BlockSpec(memory_space=pltpu.VMEM),
        scratch_shapes=[
            pltpu.VMEM((groups, BLOCK, width), bf16),
            pltpu.VMEM((groups, BLOCK, width), bf16),
            pltpu.VMEM((groups, BLOCK, LANE), bf16),
            pltpu.VMEM((groups, BLOCK, LANE), bf16),
            pltpu.VMEM((2, BLOCK, LANE), bf16),
            pltpu.VMEM((BLOCK, LANE), bf16),
            pltpu.VMEM((BLOCK, LANE), bf16),
            pltpu.VMEM((n_chunk, NBLK, BLOCK, LANE), bf16),
            pltpu.VMEM((n_chan, NBLK, BLOCK, LANE), bf16),
            pltpu.VMEM((n_chan, NBLK, BLOCK, LANE), bf16),
            pltpu.VMEM((2 * channels, wide), bf16),
            pltpu.VMEM((SHIFTS * BLOCK, wide), bf16),
            pltpu.VMEM((SHIFTS * BLOCK, LANE), f32),
            pltpu.VMEM((SHIFTS * BLOCK, LANE), f32),
            pltpu.VMEM((2, chips, ROWS, LANE), f32),
            pltpu.VMEM((chips, ROWS, LANE), f32),
            pltpu.VMEM((chips, ROWS, LANE), f32),
            pltpu.VMEM((chips, ROWS, LANE), f32),
            dma, dma((4,)), dma((4,)), dma, dma, dma, dma,
            dma((NBLK,)), dma((NBLK,)), dma, dma,
        ],
        compiler_params=pltpu.CompilerParams(
            collective_id=0, has_side_effects=True, vmem_limit_bytes=32 << 20
        ),
        name="correlate",
    )(blocks, offsets, record.reshape(groups, BLOCK, width))


def solution(mesh):
    placed = (P("chan", "tm"), P(), P("tm"))
    run = functools.partial(local, mesh.shape["chan"], mesh.shape["tm"])
    return jax.shard_map(run, mesh=mesh, in_specs=placed, out_specs=P("tm", None, "chan"), check_vma=False)
```

```python
import functools
import math

import jax
import jax.numpy as jnp
from jax import lax
from jax.experimental import pallas as pl
from jax.experimental.pallas import tpu as pltpu
from jax.sharding import PartitionSpec as P

LAG = 16
BLOCK = 16
NBLK = 4
LAGS = 33
EPS = 1e-06
LANE = 128
NX = 4
SHIFTS = LAG + 1
ROWS = 80
STEPS = 128.0
TOP = 32760.0
MESH = pl.DeviceIdType.MESH
bf16, f32 = jnp.bfloat16, jnp.float32


def shifted(before, here, count):
    if count == 0:
        return here
    lane = lax.broadcasted_iota(jnp.int32, here.shape, here.ndim - 1)
    axis = here.ndim - 1
    return jnp.where(lane < count, pltpu.roll(before, count, axis), pltpu.roll(here, count, axis))


def scale_of(code):
    return jnp.exp2(code * (1.0 / STEPS))


def kernel(
    n_chan, n_tm, blocks_hbm, offsets_hbm, record_ref, out_ref,
    blocks_ref, offsets_ref, raw, own, normed, offs, halo_out, halo, cand,
    rows_0, rows_1, rows_2, rows_3, cols_0, cols_1, cols_2, cols_3,
    srcs, both, lhs, low, high, tail, psend, p3,
    in_sem, half_send, half_recv, halo_send, halo_recv, rows_send, rows_recv, cols_send, cols_recv,
    srcs_send, srcs_recv, p3_send, p3_recv,
):
    chan = lax.axis_index("chan")
    tm = lax.axis_index("tm")
    chips = n_tm // 2
    zs = chips // 2
    core = lax.rem(tm, 2)
    chip = lax.div(tm, 2)
    other = 1 - core
    groups = raw.shape[0]
    width = raw.shape[2]
    n_chunk = width // LANE
    samples = width // 2
    beside = lax.rem(chip + chips - 1 + 2 * core, chips)
    ny = n_chan // NX
    per = n_chunk // NX
    x = lax.rem(chan, NX)
    yh = lax.div(chan, NX)
    x_peers = [lax.rem(x + d, NX) for d in (2, 1, 3)]
    y_peers = [lax.rem(yh + d, ny) for d in (2, 1, 3)]
    y = lax.div(chip, zs)
    z = lax.rem(chip, zs)
    order = (1 - y, y)
    rows_in = (rows_0, rows_1, rows_2, rows_3)
    cols_in = (cols_0, cols_1, cols_2, cols_3)

    loads = [
        pltpu.make_async_copy(record_ref, raw, in_sem.at[0]),
        pltpu.make_async_copy(blocks_hbm, blocks_ref, in_sem.at[1]),
        pltpu.make_async_copy(offsets_hbm, offsets_ref, in_sem.at[2]),
    ]
    for copy in loads:
        copy.start()

    def greet(c, t):
        pl.semaphore_signal(barrier, inc=1, device_id=(c, t), device_id_type=MESH)

    barrier = pltpu.get_barrier_semaphore()
    for peer in y_peers:
        greet(peer * NX + x, tm)
    for peer in x_peers:
        greet(yh * NX + peer, tm)
        greet(yh * NX + peer, chip * 2 + other)
    greet(chan, chip * 2 + other)
    for j in range(1, chips):
        greet(chan, lax.rem(chip + j, chips) * 2 + core)
    greet(chan, beside * 2 + other)

    for copy in loads:
        copy.wait()
    for row in range(groups):
        for window in range(2):
            cols = pl.ds(window * samples, samples)
            values = raw[row, :, cols].astype(f32)
            magnitude = jnp.mean(jnp.abs(values), axis=1, keepdims=True)
            scaled = (values / (magnitude + EPS)).astype(bf16)
            own[row, :, cols] = scaled
            normed[core, row, :, cols] = scaled

    pair = lax.div(lax.broadcasted_iota(jnp.int32, (BLOCK, width), 0), 2)
    even = lax.rem(pair, 2) == 0
    for turn, n in enumerate(order):
        first = own[lax.rem(blocks_ref[2 * n], groups)]
        second = own[lax.rem(blocks_ref[2 * n + 1], groups)]
        tiles = (
            jnp.where(even, first, pltpu.roll(second, 2, 0)),
            jnp.where(even, pltpu.roll(first, BLOCK - 2, 0), second),
        )
        for q in range(2):
            for j in range(n_chunk):
                cand[turn, j // per, q, j % per] = tiles[q][:, j * LANE : (j + 1) * LANE]
    for w in range(2):
        offs[core, w] = jnp.full((BLOCK, LANE), offsets_ref[w], jnp.int32).astype(f32).astype(bf16)
    edge_at = pl.multiple_of(core * (width - LANE), LANE)
    halo_out[0:groups] = own[:, :, pl.ds(edge_at, LANE)]
    halo_out[groups] = offs[core, core]

    pl.semaphore_wait(barrier, 2 * NX + ny + chips - 2)

    sent = []
    for turn in range(2):
        for h in range(2):
            for peer in x_peers + [x]:
                for q, t in ((core, tm), (other, chip * 2 + other)):
                    if peer is x and q is core:
                        copy = pltpu.make_async_copy(
                            cand.at[turn, x, core], rows_in[2 * turn + h].at[x], rows_recv.at[2 * turn + h]
                        )
                    else:
                        copy = pltpu.make_async_remote_copy(
                            src_ref=cand.at[turn, peer, q], dst_ref=rows_in[2 * turn + h].at[x],
                            send_sem=rows_send, recv_sem=rows_recv.at[2 * turn + h],
                            device_id=(yh * NX + peer, t), device_id_type=MESH,
                        )
                        sent.append(copy) if h == 0 else None
                    pl.when(core == h)(copy.start)

    halo_copies = [
        pltpu.make_async_remote_copy(
            src_ref=halo_out, dst_ref=halo.at[other], send_sem=halo_send.at[q], recv_sem=halo_recv.at[other],
            device_id=(chan, beside * 2 + q), device_id_type=MESH,
        )
        for q in range(2)
    ]
    half_copies = [
        pltpu.make_async_remote_copy(
            src_ref=ref.at[core], dst_ref=ref.at[core], send_sem=half_send.at[i], recv_sem=half_recv.at[i],
            device_id=(chan, chip * 2 + other), device_id_type=MESH,
        )
        for i, ref in enumerate((normed, offs))
    ]
    for copy in halo_copies + half_copies:
        copy.start()

    def mixed(first, second):
        return jnp.where(even[None, :, :LANE], first.astype(f32), second.astype(f32))

    for k in range(4):
        n = order[k // 2]
        pltpu.make_async_copy(rows_in[k], rows_in[k], rows_recv.at[k]).wait()
        first = rows_in[k][lax.rem(lax.div(blocks_ref[2 * n], groups), NX)]
        second = rows_in[k][lax.rem(lax.div(blocks_ref[2 * n + 1], groups), NX)]
        cols_in[k][yh] = mixed(first, second).astype(bf16)
        for peer in y_peers:
            copy = pltpu.make_async_remote_copy(
                src_ref=cols_in[k].at[yh], dst_ref=cols_in[k].at[yh], send_sem=cols_send, recv_sem=cols_recv.at[k],
                device_id=(peer * NX + x, tm), device_id_type=MESH,
            )
            copy.start()
            sent.append(copy)

    for copy in half_copies:
        copy.wait_recv()
    for side in range(2):
        pltpu.make_async_copy(halo.at[side], halo.at[side], halo_recv.at[side]).wait()

    at_start = chip == 0
    at_end = chip == chips - 1
    zero = jnp.zeros((BLOCK, LANE), bf16)
    for row in range(groups):
        before = jnp.where(at_start, zero, halo[0, row])
        after = jnp.where(at_end, zero, halo[1, row])
        for b in range(2 * n_chunk + 1):
            h, j = divmod(b, n_chunk)
            here = normed[h, row, :, j * LANE : (j + 1) * LANE] if h < 2 else after
            both[row * 16 : row * 16 + 16, b * LANE : (b + 1) * LANE] = shifted(before, here, LAG)
            both[LANE + row * 16 : LANE + row * 16 + 16, b * LANE : (b + 1) * LANE] = here
            before = here

    lane = lax.broadcasted_iota(jnp.int32, (per, BLOCK, LANE), 2)
    lane += lax.broadcasted_iota(jnp.int32, (per, BLOCK, LANE), 0) * LANE
    counts = []
    for h in range(2):
        at = (lane + (h * width + x * (per * LANE))).astype(f32)
        count = jnp.zeros((per, BLOCK, LANE), f32)
        for w in range(4):
            begin = offs[w // 2, w % 2].astype(f32) + float(w * samples)
            count += jnp.where((at >= begin) & (at < begin + float(samples)), 1.0, 0.0)
        reach = jnp.where(at_start, -1.0, 1.0) * 64.0
        count += jnp.where((at < halo[0, groups].astype(f32)) & (at < reach), 1.0, 0.0)
        reach = 2.0 * width - jnp.where(at_end, -1.0, 1.0) * 64.0
        count += jnp.where((at >= halo[1, groups].astype(f32) + 2.0 * width) & (at >= reach), 1.0, 0.0)
        counts.append(count)

    for k in range(4):
        n = order[k // 2]
        arrived = cols_in[k].at[pl.ds(0, ny - 1)]
        pltpu.make_async_copy(arrived, arrived, cols_recv.at[k]).wait()
        first = cols_in[k][lax.div(blocks_ref[2 * n], groups * NX)]
        second = cols_in[k][lax.div(blocks_ref[2 * n + 1], groups * NX)]
        srcs[k, x] = (mixed(first, second) * counts[k % 2]).astype(bf16)
        for peer in x_peers:
            copy = pltpu.make_async_remote_copy(
                src_ref=srcs.at[k, x], dst_ref=srcs.at[k, x], send_sem=srcs_send, recv_sem=srcs_recv.at[k],
                device_id=(yh * NX + peer, tm), device_id_type=MESH,
            )
            copy.start()
            sent.append(copy)

    for turn, n in enumerate(order):
        found = None
        for h in range(2):
            k = 2 * turn + h
            arrived = srcs.at[k, pl.ds(0, NX - 1)]
            pltpu.make_async_copy(arrived, arrived, srcs_recv.at[k]).wait()
            begin, end = h * n_chunk, (h + 1) * n_chunk + h
            for i in range(SHIFTS):
                before = srcs[k - 1, NX - 1, per - 1] if h else zero
                for b in range(begin, end):
                    j = b - begin
                    here = srcs[k, j // per, j % per] if j < n_chunk else zero
                    lhs[i * 16 : i * 16 + 16, b * LANE : (b + 1) * LANE] = shifted(before, here, i)
                    before = here
            cols = pl.ds(begin * LANE, (end - begin) * LANE)
            part = lax.dot_general(
                lhs[:, cols], both[:, cols], (((1,), (1,)), ((), ())), preferred_element_type=f32
            )
            found = part if found is None else found + part
        low[...] = found[:, :LANE]
        high[...] = found[:, LANE:]
        top = jnp.abs(high[LAG * BLOCK :])
        for i in range(LAG):
            rows = pl.ds(i * BLOCK, BLOCK)
            top = jnp.maximum(top, jnp.maximum(jnp.abs(low[rows]), jnp.abs(high[rows])))
        code = jnp.ceil(jnp.log2(jnp.maximum(top, 1e-30)) * STEPS)
        factor = TOP / scale_of(code)
        for i in range(SHIFTS):
            rows = pl.ds(i * BLOCK, BLOCK)
            if i < LAG:
                low[rows] = jnp.round(low[rows] * factor)
            high[rows] = jnp.round(high[rows] * factor)
        last = high[LAG * BLOCK :]
        for p in range(BLOCK // 2):
            tail[4 * p : 4 * p + 2] = last[2 * p : 2 * p + 2]
            tail[4 * p + 2 : 4 * p + 4] = code[2 * p : 2 * p + 2]
        for s in range(BLOCK):
            p = s // 2
            to = zs * n + (p % 2) * (zs // 2) + p // 2
            for part, ref in enumerate((low, high)):
                at_row = (s % 2) * 32 + part * 16
                psend[to, at_row : at_row + 16] = ref[pl.ds(s, 16, stride=16), :].astype(jnp.int32).astype(jnp.int16)
            if s % 2 == 0:
                psend[to, 64:80] = tail[4 * p : 4 * p + 16].astype(jnp.int32).astype(jnp.int16)
        for dz in (4, 3, 5, 2, 6, 1, 7, 0):
            to = zs * n + lax.rem(z + dz, zs)
            if turn == 1 and dz == 0:
                pltpu.make_async_copy(psend.at[to], p3.at[chip], p3_recv).start()
            else:
                pltpu.make_async_remote_copy(
                    src_ref=psend.at[to], dst_ref=p3.at[chip], send_sem=p3_send, recv_sem=p3_recv,
                    device_id=(chan, to * 2 + core), device_id_type=MESH,
                ).start()

    pltpu.make_async_copy(p3, p3, p3_recv).wait()
    sums = [jnp.zeros((32, LANE), f32)] * 2 + [jnp.zeros((1, LANE), f32)] * 2
    for j in range(chips):
        piece = p3[j].astype(jnp.int32).astype(f32)
        for s in range(2):
            scale = scale_of(piece[66 + s : 67 + s])
            sums[s] += piece[32 * s : 32 * s + 32] * scale
            sums[2 + s] += piece[64 + s : 65 + s] * scale
    final = 1.0 / (TOP * math.sqrt(n_tm * 2 * samples))
    for s in range(2):
        out_ref[s, 0:32] = sums[s] * final
        out_ref[s, 32:33] = sums[2 + s] * final

    for copy in sent + halo_copies + half_copies:
        copy.wait_send()
    gone = p3.at[pl.ds(0, chips - 1)]
    pltpu.make_async_copy(gone, gone, p3_send).wait()


def local(n_chan, n_tm, record, blocks, offsets):
    channels, width = record.shape
    groups = channels // BLOCK
    n_chunk = width // LANE
    per = n_chunk // NX
    chips = n_tm // 2
    dma = pltpu.SemaphoreType.DMA
    wide = (2 * n_chunk + 1) * LANE
    return pl.pallas_call(
        functools.partial(kernel, n_chan, n_tm),
        out_shape=jax.ShapeDtypeStruct((2, LAGS, channels), f32),
        in_specs=[pl.BlockSpec(memory_space=pltpu.HBM)] * 3,
        out_specs=pl.BlockSpec(memory_space=pltpu.VMEM),
        scratch_shapes=[
            pltpu.SMEM((NBLK,), jnp.int32),
            pltpu.SMEM((2,), jnp.int32),
            pltpu.VMEM((groups, BLOCK, width), bf16),
            pltpu.VMEM((groups, BLOCK, width), bf16),
            pltpu.VMEM((2, groups, BLOCK, width), bf16),
            pltpu.VMEM((2, 2, BLOCK, LANE), bf16),
            pltpu.VMEM((groups + 1, BLOCK, LANE), bf16),
            pltpu.VMEM((2, groups + 1, BLOCK, LANE), bf16),
            pltpu.VMEM((2, NX, 2, per, BLOCK, LANE), bf16),
            *[pltpu.VMEM((NX, per, BLOCK, LANE), bf16)] * 4,
            *[pltpu.VMEM((n_chan // NX, per, BLOCK, LANE), bf16)] * 4,
            pltpu.VMEM((4, NX, per, BLOCK, LANE), bf16),
            pltpu.VMEM((2 * channels, wide), bf16),
            pltpu.VMEM((SHIFTS * BLOCK, wide), bf16),
            pltpu.VMEM((SHIFTS * BLOCK, LANE), f32),
            pltpu.VMEM((SHIFTS * BLOCK, LANE), f32),
            pltpu.VMEM((48, LANE), f32),
            pltpu.VMEM((chips, ROWS, LANE), jnp.int16),
            pltpu.VMEM((chips, ROWS, LANE), jnp.int16),
            dma((3,)), dma((2,)), dma((2,)), dma((2,)), dma((2,)), dma, dma((4,)), dma, dma((4,)), dma, dma((4,)), dma, dma,
        ],
        compiler_params=pltpu.CompilerParams(
            collective_id=0, has_side_effects=True, vmem_limit_bytes=(60 << 20)
        ),
        name="correlate",
    )(blocks, offsets, record.reshape(groups, BLOCK, width))


def solution(mesh):
    placed = (P("chan", "tm"), P(), P("tm"))
    run = functools.partial(local, mesh.shape["chan"], mesh.shape["tm"])
    return jax.shard_map(run, mesh=mesh, in_specs=placed, out_specs=P("tm", None, "chan"), check_vma=False)
```

```python
import functools
import math

import jax
import jax.numpy as jnp
from jax import lax
from jax.experimental import pallas as pl
from jax.experimental.pallas import tpu as pltpu
from jax.sharding import PartitionSpec as P

LAG = 16
BLOCK = 16
NBLK = 4
LAGS = 33
EPS = 1e-06
LANE = 128
NX = 4
SHIFTS = LAG + 1
ROWS = 64
STEPS = 128.0
TOP = 32760.0
MESH = pl.DeviceIdType.MESH
bf16, f32 = jnp.bfloat16, jnp.float32


def shifted(before, here, count):
    if count == 0:
        return here
    lane = lax.broadcasted_iota(jnp.int32, here.shape, here.ndim - 1)
    axis = here.ndim - 1
    return jnp.where(lane < count, pltpu.roll(before, count, axis), pltpu.roll(here, count, axis))


def scale_of(code):
    return jnp.exp2(code * (1.0 / STEPS))


def kernel(
    n_chan, n_tm, blocks_hbm, offsets_hbm, record_ref, out_ref,
    blocks_ref, offsets_ref, raw, own, normed, offs, halo_out, halo, cand,
    rows_0, rows_1, rows_2, rows_3, cols_0, cols_1, cols_2, cols_3,
    srcs, both, lhs, low, high, last, last_in, psend, p3,
    in_sem, half_send, half_recv, halo_send, halo_recv, rows_send, rows_recv, cols_send, cols_recv,
    srcs_send, srcs_recv, p3_send, p3_recv, last_send, last_recv,
):
    chan = lax.axis_index("chan")
    tm = lax.axis_index("tm")
    chips = n_tm // 2
    zs = chips // 2
    core = lax.rem(tm, 2)
    chip = lax.div(tm, 2)
    other = 1 - core
    groups = raw.shape[0]
    width = raw.shape[2]
    n_chunk = width // LANE
    samples = width // 2
    beside = lax.rem(chip + chips - 1 + 2 * core, chips)
    ny = n_chan // NX
    per = n_chunk // NX
    x = lax.rem(chan, NX)
    yh = lax.div(chan, NX)
    x_peers = [lax.rem(x + d, NX) for d in (2, 1, 3)]
    y_peers = [lax.rem(yh + d, ny) for d in (2, 1, 3)]
    y = lax.div(chip, zs)
    z = lax.rem(chip, zs)
    order = (1 - y, y)
    rows_in = (rows_0, rows_1, rows_2, rows_3)
    cols_in = (cols_0, cols_1, cols_2, cols_3)

    loads = [
        pltpu.make_async_copy(record_ref, raw, in_sem.at[0]),
        pltpu.make_async_copy(blocks_hbm, blocks_ref, in_sem.at[1]),
        pltpu.make_async_copy(offsets_hbm, offsets_ref, in_sem.at[2]),
    ]
    for copy in loads:
        copy.start()

    def greet(c, t):
        pl.semaphore_signal(barrier, inc=1, device_id=(c, t), device_id_type=MESH)

    barrier = pltpu.get_barrier_semaphore()
    for peer in y_peers:
        greet(peer * NX + x, tm)
    for peer in x_peers:
        greet(yh * NX + peer, tm)
        greet(yh * NX + peer, chip * 2 + other)
    greet(chan, chip * 2 + other)
    for j in range(1, chips):
        greet(chan, lax.rem(chip + j, chips) * 2 + core)
    greet(chan, beside * 2 + other)

    for copy in loads:
        copy.wait()
    for row in range(groups):
        for window in range(2):
            cols = pl.ds(window * samples, samples)
            values = raw[row, :, cols].astype(f32)
            magnitude = jnp.mean(jnp.abs(values), axis=1, keepdims=True)
            scaled = (values / (magnitude + EPS)).astype(bf16)
            own[row, :, cols] = scaled
            normed[core, row, :, cols] = scaled

    pair = lax.div(lax.broadcasted_iota(jnp.int32, (BLOCK, width), 0), 2)
    even = lax.rem(pair, 2) == 0
    for turn, n in enumerate(order):
        first = own[lax.rem(blocks_ref[2 * n], groups)]
        second = own[lax.rem(blocks_ref[2 * n + 1], groups)]
        tiles = (
            jnp.where(even, first, pltpu.roll(second, 2, 0)),
            jnp.where(even, pltpu.roll(first, BLOCK - 2, 0), second),
        )
        for q in range(2):
            for j in range(n_chunk):
                cand[turn, j // per, q, j % per] = tiles[q][:, j * LANE : (j + 1) * LANE]
    for w in range(2):
        offs[core, w] = jnp.full((BLOCK, LANE), offsets_ref[w], jnp.int32).astype(f32).astype(bf16)
    edge_at = pl.multiple_of(core * (width - LANE), LANE)
    halo_out[0:groups] = own[:, :, pl.ds(edge_at, LANE)]
    halo_out[groups] = offs[core, core]

    pl.semaphore_wait(barrier, 2 * NX + ny + chips - 2)

    sent = []
    for turn in range(2):
        for h in range(2):
            for peer in x_peers + [x]:
                for q, t in ((core, tm), (other, chip * 2 + other)):
                    if peer is x and q is core:
                        copy = pltpu.make_async_copy(
                            cand.at[turn, x, core], rows_in[2 * turn + h].at[x], rows_recv.at[2 * turn + h]
                        )
                    else:
                        copy = pltpu.make_async_remote_copy(
                            src_ref=cand.at[turn, peer, q], dst_ref=rows_in[2 * turn + h].at[x],
                            send_sem=rows_send, recv_sem=rows_recv.at[2 * turn + h],
                            device_id=(yh * NX + peer, t), device_id_type=MESH,
                        )
                        sent.append(copy) if h == 0 else None
                    pl.when(core == h)(copy.start)

    halo_copies = [
        pltpu.make_async_remote_copy(
            src_ref=halo_out, dst_ref=halo.at[other], send_sem=halo_send.at[q], recv_sem=halo_recv.at[other],
            device_id=(chan, beside * 2 + q), device_id_type=MESH,
        )
        for q in range(2)
    ]
    half_copies = [
        pltpu.make_async_remote_copy(
            src_ref=ref.at[core], dst_ref=ref.at[core], send_sem=half_send.at[i], recv_sem=half_recv.at[i],
            device_id=(chan, chip * 2 + other), device_id_type=MESH,
        )
        for i, ref in enumerate((normed, offs))
    ]
    for copy in halo_copies + half_copies:
        copy.start()

    def mixed(first, second):
        return jnp.where(even[None, :, :LANE], first.astype(f32), second.astype(f32))

    for k in range(4):
        n = order[k // 2]
        pltpu.make_async_copy(rows_in[k], rows_in[k], rows_recv.at[k]).wait()
        first = rows_in[k][lax.rem(lax.div(blocks_ref[2 * n], groups), NX)]
        second = rows_in[k][lax.rem(lax.div(blocks_ref[2 * n + 1], groups), NX)]
        cols_in[k][yh] = mixed(first, second).astype(bf16)
        for peer in y_peers:
            copy = pltpu.make_async_remote_copy(
                src_ref=cols_in[k].at[yh], dst_ref=cols_in[k].at[yh], send_sem=cols_send, recv_sem=cols_recv.at[k],
                device_id=(peer * NX + x, tm), device_id_type=MESH,
            )
            copy.start()
            sent.append(copy)

    for copy in half_copies:
        copy.wait_recv()
    for side in range(2):
        pltpu.make_async_copy(halo.at[side], halo.at[side], halo_recv.at[side]).wait()

    at_start = chip == 0
    at_end = chip == chips - 1
    zero = jnp.zeros((BLOCK, LANE), bf16)
    for row in range(groups):
        before = jnp.where(at_start, zero, halo[0, row])
        after = jnp.where(at_end, zero, halo[1, row])
        for b in range(2 * n_chunk + 1):
            h, j = divmod(b, n_chunk)
            here = normed[h, row, :, j * LANE : (j + 1) * LANE] if h < 2 else after
            both[row * 16 : row * 16 + 16, b * LANE : (b + 1) * LANE] = shifted(before, here, LAG)
            both[LANE + row * 16 : LANE + row * 16 + 16, b * LANE : (b + 1) * LANE] = here
            before = here

    lane = lax.broadcasted_iota(jnp.int32, (per, BLOCK, LANE), 2)
    lane += lax.broadcasted_iota(jnp.int32, (per, BLOCK, LANE), 0) * LANE
    counts = []
    for h in range(2):
        at = (lane + (h * width + x * (per * LANE))).astype(f32)
        count = jnp.zeros((per, BLOCK, LANE), f32)
        for w in range(4):
            begin = offs[w // 2, w % 2].astype(f32) + float(w * samples)
            count += jnp.where((at >= begin) & (at < begin + float(samples)), 1.0, 0.0)
        reach = jnp.where(at_start, -1.0, 1.0) * 64.0
        count += jnp.where((at < halo[0, groups].astype(f32)) & (at < reach), 1.0, 0.0)
        reach = 2.0 * width - jnp.where(at_end, -1.0, 1.0) * 64.0
        count += jnp.where((at >= halo[1, groups].astype(f32) + 2.0 * width) & (at >= reach), 1.0, 0.0)
        counts.append(count)

    for k in range(4):
        n = order[k // 2]
        arrived = cols_in[k].at[pl.ds(0, ny - 1)]
        pltpu.make_async_copy(arrived, arrived, cols_recv.at[k]).wait()
        first = cols_in[k][lax.div(blocks_ref[2 * n], groups * NX)]
        second = cols_in[k][lax.div(blocks_ref[2 * n + 1], groups * NX)]
        srcs[k, x] = (mixed(first, second) * counts[k % 2]).astype(bf16)
        for peer in x_peers:
            copy = pltpu.make_async_remote_copy(
                src_ref=srcs.at[k, x], dst_ref=srcs.at[k, x], send_sem=srcs_send, recv_sem=srcs_recv.at[k],
                device_id=(yh * NX + peer, tm), device_id_type=MESH,
            )
            copy.start()
            sent.append(copy)

    for turn, n in enumerate(order):
        found = None
        for h in range(2):
            k = 2 * turn + h
            arrived = srcs.at[k, pl.ds(0, NX - 1)]
            pltpu.make_async_copy(arrived, arrived, srcs_recv.at[k]).wait()
            begin, end = h * n_chunk, (h + 1) * n_chunk + h
            for i in range(SHIFTS):
                before = srcs[k - 1, NX - 1, per - 1] if h else zero
                for b in range(begin, end):
                    j = b - begin
                    here = srcs[k, j // per, j % per] if j < n_chunk else zero
                    lhs[i * 16 : i * 16 + 16, b * LANE : (b + 1) * LANE] = shifted(before, here, i)
                    before = here
            cols = pl.ds(begin * LANE, (end - begin) * LANE)
            part = lax.dot_general(
                lhs[:, cols], both[:, cols], (((1,), (1,)), ((), ())), preferred_element_type=f32
            )
            found = part if found is None else found + part
        low[...] = found[:, :LANE]
        high[...] = found[:, LANE:]
        top = jnp.abs(high[LAG * BLOCK :])
        for i in range(LAG):
            rows = pl.ds(i * BLOCK, BLOCK)
            top = jnp.maximum(top, jnp.maximum(jnp.abs(low[rows]), jnp.abs(high[rows])))
        code = jnp.ceil(jnp.log2(jnp.maximum(top, 1e-30)) * STEPS)
        factor = TOP / scale_of(code)
        for i in range(SHIFTS):
            rows = pl.ds(i * BLOCK, BLOCK)
            if i < LAG:
                low[rows] = jnp.round(low[rows] * factor)
            high[rows] = jnp.round(high[rows] * factor)
        coded = high[LAG * BLOCK :].astype(jnp.int32) * 65536 + (code.astype(jnp.int32) + 32768)
        for s in range(BLOCK):
            p = s // 2
            to = zs * n + (p % 2) * (zs // 2) + p // 2
            for part, ref in enumerate((low, high)):
                at_row = (s % 2) * 32 + part * 16
                psend[to, at_row : at_row + 16] = ref[pl.ds(s, 16, stride=16), :].astype(jnp.int32).astype(jnp.int16)
            if s % 2 == 0:
                last[to] = coded[s : s + 2]
        for dz in (4, 3, 5, 2, 6, 1, 7, 0):
            to = zs * n + lax.rem(z + dz, zs)
            for src, dst, send, recv in ((psend, p3, p3_send, p3_recv), (last, last_in, last_send, last_recv)):
                if turn == 1 and dz == 0:
                    pltpu.make_async_copy(src.at[to], dst.at[chip], recv.at[turn]).start()
                else:
                    pltpu.make_async_remote_copy(
                        src_ref=src.at[to], dst_ref=dst.at[chip], send_sem=send, recv_sem=recv.at[turn],
                        device_id=(chan, to * 2 + core), device_id_type=MESH,
                    ).start()

    sums = [jnp.zeros((32, LANE), f32)] * 2 + [jnp.zeros((1, LANE), f32)] * 2
    for turn, n in enumerate(order):
        for ref, recv in ((p3, p3_recv), (last_in, last_recv)):
            arrived = ref.at[pl.ds(zs * n, zs)]
            pltpu.make_async_copy(arrived, arrived, recv.at[turn]).wait()
        for j in range(zs):
            piece = p3[zs * n + j].astype(jnp.int32).astype(f32)
            pair = last_in[zs * n + j]
            scales = scale_of((lax.bitwise_and(pair, 65535) - 32768).astype(f32))
            ends = lax.shift_right_arithmetic(pair, 16).astype(f32) * scales
            for s in range(2):
                sums[s] += piece[32 * s : 32 * s + 32] * scales[s : s + 1]
                sums[2 + s] += ends[s : s + 1]
    final = 1.0 / (TOP * math.sqrt(n_tm * 2 * samples))
    for s in range(2):
        out_ref[s, 0:32] = sums[s] * final
        out_ref[s, 32:33] = sums[2 + s] * final

    for copy in sent + halo_copies + half_copies:
        copy.wait_send()
    for ref, send in ((p3, p3_send), (last_in, last_send)):
        gone = ref.at[pl.ds(0, chips - 1)]
        pltpu.make_async_copy(gone, gone, send).wait()


def local(n_chan, n_tm, record, blocks, offsets):
    channels, width = record.shape
    groups = channels // BLOCK
    n_chunk = width // LANE
    per = n_chunk // NX
    chips = n_tm // 2
    dma = pltpu.SemaphoreType.DMA
    wide = (2 * n_chunk + 1) * LANE
    return pl.pallas_call(
        functools.partial(kernel, n_chan, n_tm),
        out_shape=pltpu.VMEM((2, LAGS, channels), f32),
        in_specs=[pl.BlockSpec(memory_space=pltpu.HBM)] * 3,
        out_specs=pl.BlockSpec(memory_space=pltpu.VMEM),
        scratch_shapes=[
            pltpu.SMEM((NBLK,), jnp.int32),
            pltpu.SMEM((2,), jnp.int32),
            pltpu.VMEM((groups, BLOCK, width), bf16),
            pltpu.VMEM((groups, BLOCK, width), bf16),
            pltpu.VMEM((2, groups, BLOCK, width), bf16),
            pltpu.VMEM((2, 2, BLOCK, LANE), bf16),
            pltpu.VMEM((groups + 1, BLOCK, LANE), bf16),
            pltpu.VMEM((2, groups + 1, BLOCK, LANE), bf16),
            pltpu.VMEM((2, NX, 2, per, BLOCK, LANE), bf16),
            *[pltpu.VMEM((NX, per, BLOCK, LANE), bf16)] * 4,
            *[pltpu.VMEM((n_chan // NX, per, BLOCK, LANE), bf16)] * 4,
            pltpu.VMEM((4, NX, per, BLOCK, LANE), bf16),
            pltpu.VMEM((2 * channels, wide), bf16),
            pltpu.VMEM((SHIFTS * BLOCK, wide), bf16),
            pltpu.VMEM((SHIFTS * BLOCK, LANE), f32),
            pltpu.VMEM((SHIFTS * BLOCK, LANE), f32),
            pltpu.VMEM((chips, 2, LANE), jnp.int32),
            pltpu.VMEM((chips, 2, LANE), jnp.int32),
            pltpu.VMEM((chips, ROWS, LANE), jnp.int16),
            pltpu.VMEM((chips, ROWS, LANE), jnp.int16),
            dma((3,)), dma((2,)), dma((2,)), dma((2,)), dma((2,)), dma, dma((4,)), dma, dma((4,)), dma, dma((4,)), dma, dma((2,)), dma, dma((2,)),
        ],
        compiler_params=pltpu.CompilerParams(
            collective_id=0, has_side_effects=True, vmem_limit_bytes=(24 << 20)
        ),
        name="correlate",
    )(*[pltpu.with_memory_space_constraint(a, pltpu.HBM) for a in (blocks, offsets, record.reshape(groups, BLOCK, width))])


def solution(mesh):
    placed = (P("chan", "tm"), P(), P("tm"))
    run = functools.partial(local, mesh.shape["chan"], mesh.shape["tm"])
    return jax.shard_map(run, mesh=mesh, in_specs=placed, out_specs=P("tm", None, "chan"), check_vma=False)
```

```python
import functools
import math

import jax
import jax.numpy as jnp
from jax import lax
from jax.experimental import pallas as pl
from jax.experimental.pallas import tpu as pltpu
from jax.sharding import PartitionSpec as P

LAG = 16
BLOCK = 16
NBLK = 4
LAGS = 33
EPS = 1e-06
LANE = 128
CUT = 2
NX = 4
SHIFTS = LAG + 1
ROWS = 32
STEPS = 128.0
TOP = 32760.0
MESH = pl.DeviceIdType.MESH
bf16, f32 = jnp.bfloat16, jnp.float32


def shifted(before, here, count):
    if count == 0:
        return here
    lane = lax.broadcasted_iota(jnp.int32, here.shape, here.ndim - 1)
    axis = here.ndim - 1
    return jnp.where(lane < count, pltpu.roll(before, count, axis), pltpu.roll(here, count, axis))


def whole(value):
    return jnp.round(value).astype(jnp.int32)


def upper(word):
    return lax.shift_right_arithmetic(word, 16).astype(f32)


def scale_of(code):
    return jnp.exp2(code * (1.0 / STEPS))


def kernel(
    n_chan, n_tm, blocks_hbm, offsets_hbm, record_ref, out_ref,
    blocks_ref, offsets_ref, raw, own, normed, offs, halo_out, halo, cand,
    srcs, both, lhs, low, high, paired, last, last_in, psend, p3,
    in_sem, half_send, half_recv, halo_send, halo_recv, rows_send, rows_recv, cols_send, cols_recv,
    srcs_send, srcs_recv, p3_send, p3_recv, last_send, last_recv, *landing,
):
    chan = lax.axis_index("chan")
    tm = lax.axis_index("tm")
    chips = n_tm // 2
    zs = chips // 2
    core = lax.rem(tm, 2)
    chip = lax.div(tm, 2)
    other = 1 - core
    groups = raw.shape[0]
    width = raw.shape[2]
    n_chunk = width // LANE
    samples = width // 2
    beside = lax.rem(chip + chips - 1 + 2 * core, chips)
    ny = n_chan // NX
    per = n_chunk // NX
    x = lax.rem(chan, NX)
    yh = lax.div(chan, NX)
    x_peers = [lax.rem(x + d, NX) for d in (2, 1, 3)]
    y_peers = [lax.rem(yh + d, ny) for d in (2, 1, 3)]
    y = lax.div(chip, zs)
    z = lax.rem(chip, zs)
    order = (1 - y, y)
    parts = [(turn, h, c) for turn in range(2) for h in range(2) for c in range(CUT)]
    rows_in, cols_in = landing[: len(parts)], landing[len(parts) :]
    size = per // CUT

    loads = [
        pltpu.make_async_copy(record_ref, raw, in_sem.at[0]),
        pltpu.make_async_copy(blocks_hbm, blocks_ref, in_sem.at[1]),
        pltpu.make_async_copy(offsets_hbm, offsets_ref, in_sem.at[2]),
    ]
    def greet(c, t):
        pl.semaphore_signal(barrier, inc=1, device_id=(c, t), device_id_type=MESH)

    barrier = pltpu.get_barrier_semaphore()
    spans = [(dy, dz) for dz in range(zs) for dy in range(2) if dy or dz]
    spans.sort(key=lambda d: -(d[0] + min(d[1], zs - d[1])))
    for dy, dz in spans:
        greet(chan, (lax.rem(y + dy, 2) * zs + lax.rem(z + dz, zs)) * 2 + core)
    for peer in y_peers:
        greet(peer * NX + x, tm)
    for peer in x_peers:
        greet(yh * NX + peer, tm)
        greet(yh * NX + peer, chip * 2 + other)
    greet(chan, chip * 2 + other)
    greet(chan, beside * 2 + other)
    for copy in loads:
        copy.start()

    for copy in loads:
        copy.wait()
    for row in range(groups):
        for window in range(2):
            cols = pl.ds(window * samples, samples)
            values = raw[row, :, cols].astype(f32)
            magnitude = jnp.mean(jnp.abs(values), axis=1, keepdims=True)
            scaled = (values / (magnitude + EPS)).astype(bf16)
            own[row, :, cols] = scaled
            normed[core, row, :, cols] = scaled

    pair = lax.div(lax.broadcasted_iota(jnp.int32, (BLOCK, width), 0), 2)
    even = lax.rem(pair, 2) == 0
    for turn, n in enumerate(order):
        first = own[lax.rem(blocks_ref[2 * n], groups)]
        second = own[lax.rem(blocks_ref[2 * n + 1], groups)]
        tiles = (
            jnp.where(even, first, pltpu.roll(second, 2, 0)),
            jnp.where(even, pltpu.roll(first, BLOCK - 2, 0), second),
        )
        for q in range(2):
            for j in range(n_chunk):
                cand[turn, j // per, q, j % per] = tiles[q][:, j * LANE : (j + 1) * LANE]
    for w in range(2):
        offs[core, w] = jnp.full((BLOCK, LANE), offsets_ref[w], jnp.int32).astype(f32).astype(bf16)
    edge_at = pl.multiple_of(core * (width - LANE), LANE)
    halo_out[0:groups] = own[:, :, pl.ds(edge_at, LANE)]
    halo_out[groups] = offs[core, core]

    pl.semaphore_wait(barrier, 2 * NX + ny + chips - 2)

    sent = []
    for k, (turn, h, c) in enumerate(parts):
        cut = pl.ds(c * size, size)
        for peer in x_peers + [x]:
            for q, t in ((core, tm), (other, chip * 2 + other)):
                if peer is x and q is core:
                    copy = pltpu.make_async_copy(cand.at[turn, x, core, cut], rows_in[k].at[x], rows_recv.at[k])
                else:
                    copy = pltpu.make_async_remote_copy(
                        src_ref=cand.at[turn, peer, q, cut], dst_ref=rows_in[k].at[x],
                        send_sem=rows_send, recv_sem=rows_recv.at[k],
                        device_id=(yh * NX + peer, t), device_id_type=MESH,
                    )
                    sent.append(copy) if h == 0 else None
                pl.when(core == h)(copy.start)

    halo_copies = [
        pltpu.make_async_remote_copy(
            src_ref=halo_out, dst_ref=halo.at[other], send_sem=halo_send.at[q], recv_sem=halo_recv.at[other],
            device_id=(chan, beside * 2 + q), device_id_type=MESH,
        )
        for q in range(2)
    ]
    half_copies = [
        pltpu.make_async_remote_copy(
            src_ref=ref.at[core], dst_ref=ref.at[core], send_sem=half_send.at[i], recv_sem=half_recv.at[i],
            device_id=(chan, chip * 2 + other), device_id_type=MESH,
        )
        for i, ref in enumerate((normed, offs))
    ]
    for copy in halo_copies + half_copies:
        copy.start()

    def mixed(first, second):
        return jnp.where(even[None, :, :LANE], first.astype(f32), second.astype(f32))

    for k, (turn, h, c) in enumerate(parts):
        n = order[turn]
        pltpu.make_async_copy(rows_in[k], rows_in[k], rows_recv.at[k]).wait()
        first = rows_in[k][lax.rem(lax.div(blocks_ref[2 * n], groups), NX)]
        second = rows_in[k][lax.rem(lax.div(blocks_ref[2 * n + 1], groups), NX)]
        cols_in[k][yh] = mixed(first, second).astype(bf16)
        for peer in y_peers:
            copy = pltpu.make_async_remote_copy(
                src_ref=cols_in[k].at[yh], dst_ref=cols_in[k].at[yh], send_sem=cols_send, recv_sem=cols_recv.at[k],
                device_id=(peer * NX + x, tm), device_id_type=MESH,
            )
            copy.start()
            sent.append(copy)

    for copy in half_copies:
        copy.wait_recv()
    for side in range(2):
        pltpu.make_async_copy(halo.at[side], halo.at[side], halo_recv.at[side]).wait()

    at_start = chip == 0
    at_end = chip == chips - 1
    zero = jnp.zeros((BLOCK, LANE), bf16)
    for row in range(groups):
        before = jnp.where(at_start, zero, halo[0, row])
        after = jnp.where(at_end, zero, halo[1, row])
        for b in range(2 * n_chunk + 1):
            h, j = divmod(b, n_chunk)
            here = normed[h, row, :, j * LANE : (j + 1) * LANE] if h < 2 else after
            both[row * 16 : row * 16 + 16, b * LANE : (b + 1) * LANE] = shifted(before, here, LAG)
            both[LANE + row * 16 : LANE + row * 16 + 16, b * LANE : (b + 1) * LANE] = here
            before = here

    lane = lax.broadcasted_iota(jnp.int32, (per, BLOCK, LANE), 2)
    lane += lax.broadcasted_iota(jnp.int32, (per, BLOCK, LANE), 0) * LANE
    counts = []
    for h in range(2):
        at = (lane + (h * width + x * (per * LANE))).astype(f32)
        count = jnp.zeros((per, BLOCK, LANE), f32)
        for w in range(4):
            begin = offs[w // 2, w % 2].astype(f32) + float(w * samples)
            count += jnp.where((at >= begin) & (at < begin + float(samples)), 1.0, 0.0)
        reach = jnp.where(at_start, -1.0, 1.0) * 64.0
        count += jnp.where((at < halo[0, groups].astype(f32)) & (at < reach), 1.0, 0.0)
        reach = 2.0 * width - jnp.where(at_end, -1.0, 1.0) * 64.0
        count += jnp.where((at >= halo[1, groups].astype(f32) + 2.0 * width) & (at >= reach), 1.0, 0.0)
        counts.append(count)

    for k, (turn, h, c) in enumerate(parts):
        n = order[turn]
        arrived = cols_in[k].at[pl.ds(0, ny - 1)]
        pltpu.make_async_copy(arrived, arrived, cols_recv.at[k]).wait()
        first = cols_in[k][lax.div(blocks_ref[2 * n], groups * NX)]
        second = cols_in[k][lax.div(blocks_ref[2 * n + 1], groups * NX)]
        srcs[k, x] = (mixed(first, second) * counts[h][c * size : (c + 1) * size]).astype(bf16)
        for peer in x_peers:
            copy = pltpu.make_async_remote_copy(
                src_ref=srcs.at[k, x], dst_ref=srcs.at[k, x], send_sem=srcs_send, recv_sem=srcs_recv.at[k],
                device_id=(yh * NX + peer, tm), device_id_type=MESH,
            )
            copy.start()
            sent.append(copy)

    for turn, n in enumerate(order):
        found = None
        for h in range(2):
            k = (2 * turn + h) * CUT
            for c in range(CUT):
                arrived = srcs.at[k + c, pl.ds(0, NX - 1)]
                pltpu.make_async_copy(arrived, arrived, srcs_recv.at[k + c]).wait()
            begin, end = h * n_chunk, (h + 1) * n_chunk + h
            for i in range(SHIFTS):
                before = srcs[k - 1, NX - 1, size - 1] if h else zero
                for b in range(begin, end):
                    j = b - begin
                    here = srcs[k + j % per // size, j // per, j % size] if j < n_chunk else zero
                    lhs[i * 16 : i * 16 + 16, b * LANE : (b + 1) * LANE] = shifted(before, here, i)
                    before = here
            cols = pl.ds(begin * LANE, (end - begin) * LANE)
            part = lax.dot_general(
                lhs[:, cols], both[:, cols], (((1,), (1,)), ((), ())), preferred_element_type=f32
            )
            found = part if found is None else found + part
        low[...] = found[:, :LANE]
        high[...] = found[:, LANE:]
        top = jnp.abs(high[LAG * BLOCK :])
        for i in range(LAG):
            rows = pl.ds(i * BLOCK, BLOCK)
            top = jnp.maximum(top, jnp.maximum(jnp.abs(low[rows]), jnp.abs(high[rows])))
        code = jnp.ceil(jnp.log2(jnp.maximum(top, 1e-30)) * STEPS)
        factor = TOP / scale_of(code)
        for i in range(LAG):
            rows = pl.ds(i * BLOCK, BLOCK)
            paired[rows] = whole(low[rows] * factor) * 65536 + lax.bitwise_and(whole(high[rows] * factor), 65535)
        coded = whole(high[LAG * BLOCK :] * factor) * 65536 + (code.astype(jnp.int32) + 32768)
        for s in range(BLOCK):
            p = s // 2
            to = zs * n + (p % 2) * (zs // 2) + p // 2
            at_row = (s % 2) * LAG
            psend[to, at_row : at_row + LAG] = paired[pl.ds(s, LAG, stride=BLOCK), :]
            if s % 2 == 0:
                last[to] = coded[s : s + 2]
        for dz in (4, 3, 5, 2, 6, 1, 7, 0):
            to = zs * n + lax.rem(z + dz, zs)
            for src, dst, send, recv in ((psend, p3, p3_send, p3_recv), (last, last_in, last_send, last_recv)):
                if turn == 1 and dz == 0:
                    pltpu.make_async_copy(src.at[to], dst.at[chip], recv.at[turn]).start()
                else:
                    pltpu.make_async_remote_copy(
                        src_ref=src.at[to], dst_ref=dst.at[chip], send_sem=send, recv_sem=recv.at[turn],
                        device_id=(chan, to * 2 + core), device_id_type=MESH,
                    ).start()

    sums = [jnp.zeros((ROWS, LANE), f32)] * 2 + [jnp.zeros((2, LANE), f32)]
    for turn, n in enumerate(order):
        for ref, recv in ((p3, p3_recv), (last_in, last_recv)):
            arrived = ref.at[pl.ds(zs * n, zs)]
            pltpu.make_async_copy(arrived, arrived, recv.at[turn]).wait()
        for j in range(zs):
            piece = p3[zs * n + j]
            pair = last_in[zs * n + j]
            scales = scale_of((lax.bitwise_and(pair, 65535) - 32768).astype(f32))
            spread = jnp.concatenate([jnp.broadcast_to(scales[s : s + 1], (LAG, LANE)) for s in range(2)], axis=0)
            sums[0] += upper(piece) * spread
            sums[1] += upper(piece * 65536) * spread
            sums[2] += upper(pair) * scales
    final = 1.0 / (TOP * math.sqrt(n_tm * 2 * samples))
    for s in range(2):
        out_ref[s, 0:LAG] = sums[0][s * LAG : (s + 1) * LAG] * final
        out_ref[s, LAG : 2 * LAG] = sums[1][s * LAG : (s + 1) * LAG] * final
        out_ref[s, 2 * LAG : LAGS] = sums[2][s : s + 1] * final

    for copy in sent + halo_copies + half_copies:
        copy.wait_send()
    for ref, send in ((p3, p3_send), (last_in, last_send)):
        gone = ref.at[pl.ds(0, chips - 1)]
        pltpu.make_async_copy(gone, gone, send).wait()


def local(n_chan, n_tm, record, blocks, offsets):
    channels, width = record.shape
    groups = channels // BLOCK
    n_chunk = width // LANE
    per = n_chunk // NX
    chips = n_tm // 2
    dma = pltpu.SemaphoreType.DMA
    wide = (2 * n_chunk + 1) * LANE
    return pl.pallas_call(
        functools.partial(kernel, n_chan, n_tm),
        out_shape=pltpu.VMEM((2, LAGS, channels), f32),
        in_specs=[pl.BlockSpec(memory_space=pltpu.HBM)] * 3,
        out_specs=pl.BlockSpec(memory_space=pltpu.VMEM),
        scratch_shapes=[
            pltpu.SMEM((NBLK,), jnp.int32),
            pltpu.SMEM((2,), jnp.int32),
            pltpu.VMEM((groups, BLOCK, width), bf16),
            pltpu.VMEM((groups, BLOCK, width), bf16),
            pltpu.VMEM((2, groups, BLOCK, width), bf16),
            pltpu.VMEM((2, 2, BLOCK, LANE), bf16),
            pltpu.VMEM((groups + 1, BLOCK, LANE), bf16),
            pltpu.VMEM((2, groups + 1, BLOCK, LANE), bf16),
            pltpu.VMEM((2, NX, 2, per, BLOCK, LANE), bf16),
            pltpu.VMEM((4 * CUT, NX, per // CUT, BLOCK, LANE), bf16),
            pltpu.VMEM((2 * channels, wide), bf16),
            pltpu.VMEM((SHIFTS * BLOCK, wide), bf16),
            pltpu.VMEM((SHIFTS * BLOCK, LANE), f32),
            pltpu.VMEM((SHIFTS * BLOCK, LANE), f32),
            pltpu.VMEM((LAG * BLOCK, LANE), jnp.int32),
            pltpu.VMEM((chips, 2, LANE), jnp.int32),
            pltpu.VMEM((chips, 2, LANE), jnp.int32),
            pltpu.VMEM((chips, ROWS, LANE), jnp.int32),
            pltpu.VMEM((chips, ROWS, LANE), jnp.int32),
            dma((3,)), dma((2,)), dma((2,)), dma((2,)), dma((2,)), dma, dma((4 * CUT,)), dma, dma((4 * CUT,)),
            dma, dma((4 * CUT,)), dma, dma((2,)), dma, dma((2,)),
            *[pltpu.VMEM((NX, per // CUT, BLOCK, LANE), bf16)] * (4 * CUT),
            *[pltpu.VMEM((n_chan // NX, per // CUT, BLOCK, LANE), bf16)] * (4 * CUT),
        ],
        compiler_params=pltpu.CompilerParams(
            collective_id=0, has_side_effects=True, vmem_limit_bytes=(24 << 20)
        ),
        name="correlate",
    )(*[pltpu.with_memory_space_constraint(a, pltpu.HBM) for a in (blocks, offsets, record.reshape(groups, BLOCK, width))])


def solution(mesh):
    placed = (P("chan", "tm"), P(), P("tm"))
    run = functools.partial(local, mesh.shape["chan"], mesh.shape["tm"])
    return jax.shard_map(run, mesh=mesh, in_specs=placed, out_specs=P("tm", None, "chan"), check_vma=False)
```

```python
import functools
import math

import jax
import jax.numpy as jnp
from jax import lax
from jax.experimental import pallas as pl
from jax.experimental.pallas import tpu as pltpu
from jax.sharding import PartitionSpec as P

LAG = 16
BLOCK = 16
NBLK = 4
LAGS = 33
EPS = 1e-06
LANE = 128
CUT = 2
NX = 4
SHIFTS = LAG + 1
ROWS = 32
STEPS = 128.0
TOP = 32760.0
MESH = pl.DeviceIdType.MESH
bf16, f32 = jnp.bfloat16, jnp.float32


def shifted(before, here, count):
    if count == 0:
        return here
    lane = lax.broadcasted_iota(jnp.int32, here.shape, here.ndim - 1)
    axis = here.ndim - 1
    return jnp.where(lane < count, pltpu.roll(before, count, axis), pltpu.roll(here, count, axis))


def whole(value):
    return jnp.round(value).astype(jnp.int32)


def upper(word):
    return lax.shift_right_arithmetic(word, 16).astype(f32)


def scale_of(code):
    return jnp.exp2(code * (1.0 / STEPS))


def kernel(
    n_chan, n_tm, blocks_hbm, offsets_hbm, record_ref, out_ref,
    blocks_ref, offsets_ref, raw, own, normed, offs, halo_out, halo, cand,
    srcs, both, lhs, low, high, paired, last, last_in, psend, p3,
    in_sem, half_send, half_recv, halo_send, halo_recv, rows_send, rows_recv, cols_send, cols_recv,
    srcs_send, srcs_recv, p3_send, p3_recv, last_send, last_recv, *landing,
):
    chan = lax.axis_index("chan")
    tm = lax.axis_index("tm")
    chips = n_tm // 2
    zs = chips // 2
    core = lax.rem(tm, 2)
    chip = lax.div(tm, 2)
    other = 1 - core
    groups = raw.shape[0]
    width = raw.shape[2]
    n_chunk = width // LANE
    samples = width // 2
    beside = lax.rem(chip + chips - 1 + 2 * core, chips)
    ny = n_chan // NX
    per = n_chunk // NX
    x = lax.rem(chan, NX)
    yh = lax.div(chan, NX)
    x_peers = [lax.rem(x + d, NX) for d in (2, 1, 3)]
    y_peers = [lax.rem(yh + d, ny) for d in (2, 1, 3)]
    y = lax.div(chip, zs)
    z = lax.rem(chip, zs)
    order = (y, 1 - y)
    parts = [(turn, h, c) for turn in range(2) for h in range(2) for c in range(CUT)]
    rows_in, cols_in = landing[: len(parts)], landing[len(parts) :]
    size = per // CUT

    loads = [
        pltpu.make_async_copy(record_ref, raw, in_sem.at[0]),
        pltpu.make_async_copy(blocks_hbm, blocks_ref, in_sem.at[1]),
        pltpu.make_async_copy(offsets_hbm, offsets_ref, in_sem.at[2]),
    ]
    def greet(c, t):
        pl.semaphore_signal(barrier, inc=1, device_id=(c, t), device_id_type=MESH)

    barrier = pltpu.get_barrier_semaphore()
    spans = [(dy, dz) for dz in range(zs) for dy in range(2) if dy or dz]
    spans.sort(key=lambda d: -(d[0] + min(d[1], zs - d[1])))
    for dy, dz in spans:
        greet(chan, (lax.rem(y + dy, 2) * zs + lax.rem(z + dz, zs)) * 2 + core)
    for peer in y_peers:
        greet(peer * NX + x, tm)
    for peer in x_peers:
        greet(yh * NX + peer, tm)
        greet(yh * NX + peer, chip * 2 + other)
    greet(chan, chip * 2 + other)
    greet(chan, beside * 2 + other)
    for copy in loads:
        copy.start()

    for copy in loads:
        copy.wait()
    for row in range(groups):
        for window in range(2):
            cols = pl.ds(window * samples, samples)
            values = raw[row, :, cols].astype(f32)
            magnitude = jnp.mean(jnp.abs(values), axis=1, keepdims=True)
            scaled = (values / (magnitude + EPS)).astype(bf16)
            own[row, :, cols] = scaled
            normed[core, row, :, cols] = scaled

    pair = lax.div(lax.broadcasted_iota(jnp.int32, (BLOCK, width), 0), 2)
    even = lax.rem(pair, 2) == 0
    for turn, n in enumerate(order):
        first = own[lax.rem(blocks_ref[2 * n], groups)]
        second = own[lax.rem(blocks_ref[2 * n + 1], groups)]
        tiles = (
            jnp.where(even, first, pltpu.roll(second, 2, 0)),
            jnp.where(even, pltpu.roll(first, BLOCK - 2, 0), second),
        )
        for q in range(2):
            for j in range(n_chunk):
                cand[turn, j // per, q, j % per] = tiles[q][:, j * LANE : (j + 1) * LANE]
    for w in range(2):
        offs[core, w] = jnp.full((BLOCK, LANE), offsets_ref[w], jnp.int32).astype(f32).astype(bf16)
    edge_at = pl.multiple_of(core * (width - LANE), LANE)
    halo_out[0:groups] = own[:, :, pl.ds(edge_at, LANE)]
    halo_out[groups] = offs[core, core]

    pl.semaphore_wait(barrier, 2 * NX + ny + chips - 2)

    sent = []
    for k, (turn, h, c) in enumerate(parts):
        cut = pl.ds(c * size, size)
        for peer in x_peers + [x]:
            for q, t in ((core, tm), (other, chip * 2 + other)):
                if peer is x and q is core:
                    copy = pltpu.make_async_copy(cand.at[turn, x, core, cut], rows_in[k].at[x], rows_recv.at[k])
                else:
                    copy = pltpu.make_async_remote_copy(
                        src_ref=cand.at[turn, peer, q, cut], dst_ref=rows_in[k].at[x],
                        send_sem=rows_send, recv_sem=rows_recv.at[k],
                        device_id=(yh * NX + peer, t), device_id_type=MESH,
                    )
                    sent.append(copy) if h == 0 else None
                pl.when(core == h)(copy.start)

    halo_copies = [
        pltpu.make_async_remote_copy(
            src_ref=halo_out, dst_ref=halo.at[other], send_sem=halo_send.at[q], recv_sem=halo_recv.at[other],
            device_id=(chan, beside * 2 + q), device_id_type=MESH,
        )
        for q in range(2)
    ]
    half_copies = [
        pltpu.make_async_remote_copy(
            src_ref=ref.at[core], dst_ref=ref.at[core], send_sem=half_send.at[i], recv_sem=half_recv.at[i],
            device_id=(chan, chip * 2 + other), device_id_type=MESH,
        )
        for i, ref in enumerate((normed, offs))
    ]
    for copy in halo_copies + half_copies:
        copy.start()

    def mixed(first, second):
        return jnp.where(even[None, :, :LANE], first.astype(f32), second.astype(f32))

    for k, (turn, h, c) in enumerate(parts):
        n = order[turn]
        pltpu.make_async_copy(rows_in[k], rows_in[k], rows_recv.at[k]).wait()
        first = rows_in[k][lax.rem(lax.div(blocks_ref[2 * n], groups), NX)]
        second = rows_in[k][lax.rem(lax.div(blocks_ref[2 * n + 1], groups), NX)]
        cols_in[k][yh] = mixed(first, second).astype(bf16)
        for peer in y_peers:
            copy = pltpu.make_async_remote_copy(
                src_ref=cols_in[k].at[yh], dst_ref=cols_in[k].at[yh], send_sem=cols_send, recv_sem=cols_recv.at[k],
                device_id=(peer * NX + x, tm), device_id_type=MESH,
            )
            copy.start()
            sent.append(copy)

    for copy in half_copies:
        copy.wait_recv()
    for side in range(2):
        pltpu.make_async_copy(halo.at[side], halo.at[side], halo_recv.at[side]).wait()

    at_start = chip == 0
    at_end = chip == chips - 1
    zero = jnp.zeros((BLOCK, LANE), bf16)
    for row in range(groups):
        before = jnp.where(at_start, zero, halo[0, row])
        after = jnp.where(at_end, zero, halo[1, row])
        for b in range(2 * n_chunk + 1):
            h, j = divmod(b, n_chunk)
            here = normed[h, row, :, j * LANE : (j + 1) * LANE] if h < 2 else after
            both[row * 16 : row * 16 + 16, b * LANE : (b + 1) * LANE] = shifted(before, here, LAG)
            both[LANE + row * 16 : LANE + row * 16 + 16, b * LANE : (b + 1) * LANE] = here
            before = here

    lane = lax.broadcasted_iota(jnp.int32, (per, BLOCK, LANE), 2)
    lane += lax.broadcasted_iota(jnp.int32, (per, BLOCK, LANE), 0) * LANE
    counts = []
    for h in range(2):
        at = (lane + (h * width + x * (per * LANE))).astype(f32)
        count = jnp.zeros((per, BLOCK, LANE), f32)
        for w in range(4):
            begin = offs[w // 2, w % 2].astype(f32) + float(w * samples)
            count += jnp.where((at >= begin) & (at < begin + float(samples)), 1.0, 0.0)
        reach = jnp.where(at_start, -1.0, 1.0) * 64.0
        count += jnp.where((at < halo[0, groups].astype(f32)) & (at < reach), 1.0, 0.0)
        reach = 2.0 * width - jnp.where(at_end, -1.0, 1.0) * 64.0
        count += jnp.where((at >= halo[1, groups].astype(f32) + 2.0 * width) & (at >= reach), 1.0, 0.0)
        counts.append(count)

    for k, (turn, h, c) in enumerate(parts):
        n = order[turn]
        arrived = cols_in[k].at[pl.ds(0, ny - 1)]
        pltpu.make_async_copy(arrived, arrived, cols_recv.at[k]).wait()
        first = cols_in[k][lax.div(blocks_ref[2 * n], groups * NX)]
        second = cols_in[k][lax.div(blocks_ref[2 * n + 1], groups * NX)]
        srcs[k, x] = (mixed(first, second) * counts[h][c * size : (c + 1) * size]).astype(bf16)
        for peer in x_peers:
            copy = pltpu.make_async_remote_copy(
                src_ref=srcs.at[k, x], dst_ref=srcs.at[k, x], send_sem=srcs_send, recv_sem=srcs_recv.at[k],
                device_id=(yh * NX + peer, tm), device_id_type=MESH,
            )
            copy.start()
            sent.append(copy)

    for turn, n in enumerate(order):
        found = None
        for h in range(2):
            k = (2 * turn + h) * CUT
            for c in range(CUT):
                arrived = srcs.at[k + c, pl.ds(0, NX - 1)]
                pltpu.make_async_copy(arrived, arrived, srcs_recv.at[k + c]).wait()
            begin, end = h * n_chunk, (h + 1) * n_chunk + h
            for i in range(SHIFTS):
                before = srcs[k - 1, NX - 1, size - 1] if h else zero
                for b in range(begin, end):
                    j = b - begin
                    here = srcs[k + j % per // size, j // per, j % size] if j < n_chunk else zero
                    lhs[i * 16 : i * 16 + 16, b * LANE : (b + 1) * LANE] = shifted(before, here, i)
                    before = here
            cols = pl.ds(begin * LANE, (end - begin) * LANE)
            part = lax.dot_general(
                lhs[:, cols], both[:, cols], (((1,), (1,)), ((), ())), preferred_element_type=f32
            )
            found = part if found is None else found + part
        low[...] = found[:, :LANE]
        high[...] = found[:, LANE:]
        top = jnp.abs(high[LAG * BLOCK :])
        for i in range(LAG):
            rows = pl.ds(i * BLOCK, BLOCK)
            top = jnp.maximum(top, jnp.maximum(jnp.abs(low[rows]), jnp.abs(high[rows])))
        code = jnp.ceil(jnp.log2(jnp.maximum(top, 1e-30)) * STEPS)
        factor = TOP / scale_of(code)
        for i in range(LAG):
            rows = pl.ds(i * BLOCK, BLOCK)
            paired[rows] = whole(low[rows] * factor) * 65536 + lax.bitwise_and(whole(high[rows] * factor), 65535)
        coded = whole(high[LAG * BLOCK :] * factor) * 65536 + (code.astype(jnp.int32) + 32768)
        for s in range(BLOCK):
            p = s // 2
            to = zs * n + (p % 2) * (zs // 2) + p // 2
            at_row = (s % 2) * LAG
            psend[to, at_row : at_row + LAG] = paired[pl.ds(s, LAG, stride=BLOCK), :]
            if s % 2 == 0:
                last[to] = coded[s : s + 2]
        for dz in (4, 3, 5, 2, 6, 1, 7, 0):
            to = zs * n + lax.rem(z + dz, zs)
            for src, dst, send, recv in ((psend, p3, p3_send, p3_recv), (last, last_in, last_send, last_recv)):
                if turn == 0 and dz == 0:
                    pltpu.make_async_copy(src.at[to], dst.at[chip], recv.at[turn]).start()
                else:
                    pltpu.make_async_remote_copy(
                        src_ref=src.at[to], dst_ref=dst.at[chip], send_sem=send, recv_sem=recv.at[turn],
                        device_id=(chan, to * 2 + core), device_id_type=MESH,
                    ).start()

    sums = [jnp.zeros((ROWS, LANE), f32)] * 2 + [jnp.zeros((2, LANE), f32)]
    for turn, n in enumerate(order):
        for ref, recv in ((p3, p3_recv), (last_in, last_recv)):
            arrived = ref.at[pl.ds(zs * n, zs)]
            pltpu.make_async_copy(arrived, arrived, recv.at[turn]).wait()
        for j in range(zs):
            piece = p3[zs * n + j]
            pair = last_in[zs * n + j]
            scales = scale_of((lax.bitwise_and(pair, 65535) - 32768).astype(f32))
            spread = jnp.concatenate([jnp.broadcast_to(scales[s : s + 1], (LAG, LANE)) for s in range(2)], axis=0)
            sums[0] += upper(piece) * spread
            sums[1] += upper(piece * 65536) * spread
            sums[2] += upper(pair) * scales
    final = 1.0 / (TOP * math.sqrt(n_tm * 2 * samples))
    for s in range(2):
        out_ref[s, 0:LAG] = sums[0][s * LAG : (s + 1) * LAG] * final
        out_ref[s, LAG : 2 * LAG] = sums[1][s * LAG : (s + 1) * LAG] * final
        out_ref[s, 2 * LAG : LAGS] = sums[2][s : s + 1] * final

    for copy in sent + halo_copies + half_copies:
        copy.wait_send()
    for ref, send in ((p3, p3_send), (last_in, last_send)):
        gone = ref.at[pl.ds(0, chips - 1)]
        pltpu.make_async_copy(gone, gone, send).wait()


def local(n_chan, n_tm, record, blocks, offsets):
    channels, width = record.shape
    groups = channels // BLOCK
    n_chunk = width // LANE
    per = n_chunk // NX
    chips = n_tm // 2
    dma = pltpu.SemaphoreType.DMA
    wide = (2 * n_chunk + 1) * LANE
    return pl.pallas_call(
        functools.partial(kernel, n_chan, n_tm),
        out_shape=pltpu.VMEM((2, LAGS, channels), f32),
        in_specs=[pl.BlockSpec(memory_space=pltpu.HBM)] * 3,
        out_specs=pl.BlockSpec(memory_space=pltpu.VMEM),
        scratch_shapes=[
            pltpu.SMEM((NBLK,), jnp.int32),
            pltpu.SMEM((2,), jnp.int32),
            pltpu.VMEM((groups, BLOCK, width), bf16),
            pltpu.VMEM((groups, BLOCK, width), bf16),
            pltpu.VMEM((2, groups, BLOCK, width), bf16),
            pltpu.VMEM((2, 2, BLOCK, LANE), bf16),
            pltpu.VMEM((groups + 1, BLOCK, LANE), bf16),
            pltpu.VMEM((2, groups + 1, BLOCK, LANE), bf16),
            pltpu.VMEM((2, NX, 2, per, BLOCK, LANE), bf16),
            pltpu.VMEM((4 * CUT, NX, per // CUT, BLOCK, LANE), bf16),
            pltpu.VMEM((2 * channels, wide), bf16),
            pltpu.VMEM((SHIFTS * BLOCK, wide), bf16),
            pltpu.VMEM((SHIFTS * BLOCK, LANE), f32),
            pltpu.VMEM((SHIFTS * BLOCK, LANE), f32),
            pltpu.VMEM((LAG * BLOCK, LANE), jnp.int32),
            pltpu.VMEM((chips, 2, LANE), jnp.int32),
            pltpu.VMEM((chips, 2, LANE), jnp.int32),
            pltpu.VMEM((chips, ROWS, LANE), jnp.int32),
            pltpu.VMEM((chips, ROWS, LANE), jnp.int32),
            dma((3,)), dma((2,)), dma((2,)), dma((2,)), dma((2,)), dma, dma((4 * CUT,)), dma, dma((4 * CUT,)),
            dma, dma((4 * CUT,)), dma, dma((2,)), dma, dma((2,)),
            *[pltpu.VMEM((NX, per // CUT, BLOCK, LANE), bf16)] * (4 * CUT),
            *[pltpu.VMEM((n_chan // NX, per // CUT, BLOCK, LANE), bf16)] * (4 * CUT),
        ],
        compiler_params=pltpu.CompilerParams(
            collective_id=0, has_side_effects=True, vmem_limit_bytes=(24 << 20)
        ),
        name="correlate",
    )(*[pltpu.with_memory_space_constraint(a, pltpu.HBM) for a in (blocks, offsets, record.reshape(groups, BLOCK, width))])


def solution(mesh):
    placed = (P("chan", "tm"), P(), P("tm"))
    run = functools.partial(local, mesh.shape["chan"], mesh.shape["tm"])
    return jax.shard_map(run, mesh=mesh, in_specs=placed, out_specs=P("tm", None, "chan"), check_vma=False)
```

```python
import functools
import math

import jax
import jax.numpy as jnp
from jax import lax
from jax.experimental import pallas as pl
from jax.experimental.pallas import tpu as pltpu
from jax.sharding import PartitionSpec as P

LAG = 16
BLOCK = 16
NBLK = 4
LAGS = 33
EPS = 1e-06
LANE = 128
CUT = 2
NX = 4
SHIFTS = LAG + 1
ROWS = 32
STEPS = 128.0
TOP = 32760.0
MESH = pl.DeviceIdType.MESH
bf16, f32 = jnp.bfloat16, jnp.float32


def shifted(before, here, count):
    if count == 0:
        return here
    lane = lax.broadcasted_iota(jnp.int32, here.shape, here.ndim - 1)
    axis = here.ndim - 1
    return jnp.where(lane < count, pltpu.roll(before, count, axis), pltpu.roll(here, count, axis))


def whole(value):
    return jnp.round(value).astype(jnp.int32)


def upper(word):
    return lax.shift_right_arithmetic(word, 16).astype(f32)


def scale_of(code):
    return jnp.exp2(code * (1.0 / STEPS))


def kernel(
    n_chan, n_tm, blocks_hbm, offsets_hbm, record_ref, out_ref,
    blocks_ref, offsets_ref, raw, own, normed, offs, halo_out, halo, cand,
    srcs, both, lhs, low, high, paired, last, last_in, psend, p3,
    in_sem, half_send, half_recv, halo_send, halo_recv, rows_send, rows_recv, cols_send, cols_recv,
    srcs_send, srcs_recv, p3_send, p3_recv, last_send, last_recv, *landing,
):
    chan = lax.axis_index("chan")
    tm = lax.axis_index("tm")
    chips = n_tm // 2
    zs = chips // 2
    core = lax.rem(tm, 2)
    chip = lax.div(tm, 2)
    other = 1 - core
    groups = raw.shape[0]
    width = raw.shape[2]
    n_chunk = width // LANE
    samples = width // 2
    beside = lax.rem(chip + chips - 1 + 2 * core, chips)
    ny = n_chan // NX
    per = n_chunk // NX
    x = lax.rem(chan, NX)
    yh = lax.div(chan, NX)
    x_peers = [lax.rem(x + d, NX) for d in (2, 1, 3)]
    y_peers = [lax.rem(yh + d, ny) for d in (2, 1, 3)]
    y = lax.div(chip, zs)
    z = lax.rem(chip, zs)
    order = (y, 1 - y)
    parts = [(turn, h, c) for turn in range(2) for h in range(2) for c in range(CUT)]
    rows_in, cols_in = landing[: len(parts)], landing[len(parts) :]
    size = per // CUT

    loads = [
        pltpu.make_async_copy(record_ref, raw, in_sem.at[0]),
        pltpu.make_async_copy(blocks_hbm, blocks_ref, in_sem.at[1]),
        pltpu.make_async_copy(offsets_hbm, offsets_ref, in_sem.at[2]),
    ]
    def greet(c, t):
        pl.semaphore_signal(barrier, inc=1, device_id=(c, t), device_id_type=MESH)

    barrier = pltpu.get_barrier_semaphore()
    spans = [(dy, dz) for dz in range(zs) for dy in range(2) if dy or dz]
    spans.sort(key=lambda d: -(d[0] + min(d[1], zs - d[1])))
    for dy, dz in spans:
        greet(chan, (lax.rem(y + dy, 2) * zs + lax.rem(z + dz, zs)) * 2 + core)
    for peer in y_peers:
        greet(peer * NX + x, tm)
    for peer in x_peers:
        greet(yh * NX + peer, tm)
        greet(yh * NX + peer, chip * 2 + other)
    greet(chan, chip * 2 + other)
    greet(chan, beside * 2 + other)
    for copy in loads:
        copy.start()

    for copy in loads:
        copy.wait()
    for row in range(groups):
        for window in range(2):
            cols = pl.ds(window * samples, samples)
            values = raw[row, :, cols].astype(f32)
            magnitude = jnp.mean(jnp.abs(values), axis=1, keepdims=True)
            scaled = (values / (magnitude + EPS)).astype(bf16)
            own[row, :, cols] = scaled
            normed[core, row, :, cols] = scaled

    pair = lax.div(lax.broadcasted_iota(jnp.int32, (BLOCK, width), 0), 2)
    even = lax.rem(pair, 2) == 0
    for turn, n in enumerate(order):
        first = own[lax.rem(blocks_ref[2 * n], groups)]
        second = own[lax.rem(blocks_ref[2 * n + 1], groups)]
        tiles = (
            jnp.where(even, first, pltpu.roll(second, 2, 0)),
            jnp.where(even, pltpu.roll(first, BLOCK - 2, 0), second),
        )
        for q in range(2):
            for j in range(n_chunk):
                cand[turn, j // per, q, j % per] = tiles[q][:, j * LANE : (j + 1) * LANE]
    for w in range(2):
        offs[core, w] = jnp.full((BLOCK, LANE), offsets_ref[w], jnp.int32).astype(f32).astype(bf16)
    edge_at = pl.multiple_of(core * (width - LANE), LANE)
    halo_out[0:groups] = own[:, :, pl.ds(edge_at, LANE)]
    halo_out[groups] = offs[core, core]

    pl.semaphore_wait(barrier, 2 * NX + ny + chips - 2)

    sent = []
    for k, (turn, h, c) in enumerate(parts):
        cut = pl.ds(c * size, size)
        for peer in x_peers + [x]:
            for q, t in ((core, tm), (other, chip * 2 + other)):
                if peer is x and q is core:
                    copy = pltpu.make_async_copy(cand.at[turn, x, core, cut], rows_in[k].at[x], rows_recv.at[k])
                else:
                    copy = pltpu.make_async_remote_copy(
                        src_ref=cand.at[turn, peer, q, cut], dst_ref=rows_in[k].at[x],
                        send_sem=rows_send, recv_sem=rows_recv.at[k],
                        device_id=(yh * NX + peer, t), device_id_type=MESH,
                    )
                    sent.append(copy) if h == 0 else None
                pl.when(core == h)(copy.start)

    halo_copies = [
        pltpu.make_async_remote_copy(
            src_ref=halo_out, dst_ref=halo.at[other], send_sem=halo_send.at[q], recv_sem=halo_recv.at[other],
            device_id=(chan, beside * 2 + q), device_id_type=MESH,
        )
        for q in range(2)
    ]
    half_copies = [
        pltpu.make_async_remote_copy(
            src_ref=ref.at[core], dst_ref=ref.at[core], send_sem=half_send.at[i], recv_sem=half_recv.at[i],
            device_id=(chan, chip * 2 + other), device_id_type=MESH,
        )
        for i, ref in enumerate((normed, offs))
    ]
    for copy in halo_copies + half_copies:
        copy.start()

    def mixed(first, second):
        return jnp.where(even[None, :, :LANE], first.astype(f32), second.astype(f32))

    for k, (turn, h, c) in enumerate(parts):
        n = order[turn]
        pltpu.make_async_copy(rows_in[k], rows_in[k], rows_recv.at[k]).wait()
        first = rows_in[k][lax.rem(lax.div(blocks_ref[2 * n], groups), NX)]
        second = rows_in[k][lax.rem(lax.div(blocks_ref[2 * n + 1], groups), NX)]
        cols_in[k][yh] = mixed(first, second).astype(bf16)
        for peer in y_peers:
            copy = pltpu.make_async_remote_copy(
                src_ref=cols_in[k].at[yh], dst_ref=cols_in[k].at[yh], send_sem=cols_send, recv_sem=cols_recv.at[k],
                device_id=(peer * NX + x, tm), device_id_type=MESH,
            )
            copy.start()
            sent.append(copy)

    for copy in half_copies:
        copy.wait_recv()
    for side in range(2):
        pltpu.make_async_copy(halo.at[side], halo.at[side], halo_recv.at[side]).wait()

    at_start = chip == 0
    at_end = chip == chips - 1
    zero = jnp.zeros((BLOCK, LANE), bf16)
    for row in range(groups):
        before = jnp.where(at_start, zero, halo[0, row])
        after = jnp.where(at_end, zero, halo[1, row])
        for b in range(2 * n_chunk + 1):
            h, j = divmod(b, n_chunk)
            here = normed[h, row, :, j * LANE : (j + 1) * LANE] if h < 2 else after
            both[row * 16 : row * 16 + 16, b * LANE : (b + 1) * LANE] = shifted(before, here, LAG)
            both[LANE + row * 16 : LANE + row * 16 + 16, b * LANE : (b + 1) * LANE] = here
            before = here

    lane = lax.broadcasted_iota(jnp.int32, (per, BLOCK, LANE), 2)
    lane += lax.broadcasted_iota(jnp.int32, (per, BLOCK, LANE), 0) * LANE
    counts = []
    for h in range(2):
        at = (lane + (h * width + x * (per * LANE))).astype(f32)
        count = jnp.zeros((per, BLOCK, LANE), f32)
        for w in range(4):
            begin = offs[w // 2, w % 2].astype(f32) + float(w * samples)
            count += jnp.where((at >= begin) & (at < begin + float(samples)), 1.0, 0.0)
        reach = jnp.where(at_start, -1.0, 1.0) * 64.0
        count += jnp.where((at < halo[0, groups].astype(f32)) & (at < reach), 1.0, 0.0)
        reach = 2.0 * width - jnp.where(at_end, -1.0, 1.0) * 64.0
        count += jnp.where((at >= halo[1, groups].astype(f32) + 2.0 * width) & (at >= reach), 1.0, 0.0)
        counts.append(count)

    for k, (turn, h, c) in enumerate(parts):
        n = order[turn]
        arrived = cols_in[k].at[pl.ds(0, ny - 1)]
        pltpu.make_async_copy(arrived, arrived, cols_recv.at[k]).wait()
        first = cols_in[k][lax.div(blocks_ref[2 * n], groups * NX)]
        second = cols_in[k][lax.div(blocks_ref[2 * n + 1], groups * NX)]
        srcs[k, x] = (mixed(first, second) * counts[h][c * size : (c + 1) * size]).astype(bf16)
        for peer in x_peers:
            copy = pltpu.make_async_remote_copy(
                src_ref=srcs.at[k, x], dst_ref=srcs.at[k, x], send_sem=srcs_send, recv_sem=srcs_recv.at[k],
                device_id=(yh * NX + peer, tm), device_id_type=MESH,
            )
            copy.start()
            sent.append(copy)

    for turn, n in enumerate(order):
        found = None
        for h in range(2):
            k = (2 * turn + h) * CUT
            for c in range(CUT):
                arrived = srcs.at[k + c, pl.ds(0, NX - 1)]
                pltpu.make_async_copy(arrived, arrived, srcs_recv.at[k + c]).wait()
            begin, end = h * n_chunk, (h + 1) * n_chunk + h
            for i in range(SHIFTS):
                before = srcs[k - 1, NX - 1, size - 1] if h else zero
                for b in range(begin, end):
                    j = b - begin
                    here = srcs[k + j % per // size, j // per, j % size] if j < n_chunk else zero
                    lhs[i * 16 : i * 16 + 16, b * LANE : (b + 1) * LANE] = shifted(before, here, i)
                    before = here
            cols = pl.ds(begin * LANE, (end - begin) * LANE)
            part = lax.dot_general(
                lhs[:, cols], both[:, cols], (((1,), (1,)), ((), ())), preferred_element_type=f32
            )
            found = part if found is None else found + part
        low[...] = found[:, :LANE]
        high[...] = found[:, LANE:]
        top = jnp.abs(high[LAG * BLOCK :])
        for i in range(LAG):
            rows = pl.ds(i * BLOCK, BLOCK)
            top = jnp.maximum(top, jnp.maximum(jnp.abs(low[rows]), jnp.abs(high[rows])))
        code = jnp.ceil(jnp.log2(jnp.maximum(top, 1e-30)) * STEPS)
        factor = TOP / scale_of(code)
        for i in range(LAG):
            rows = pl.ds(i * BLOCK, BLOCK)
            paired[rows] = whole(low[rows] * factor) * 65536 + lax.bitwise_and(whole(high[rows] * factor), 65535)
        coded = whole(high[LAG * BLOCK :] * factor) * 65536 + (code.astype(jnp.int32) + 32768)
        for s in range(BLOCK):
            p = s // 2
            to = zs * n + (p % 2) * (zs // 2) + p // 2
            at_row = (s % 2) * LAG
            psend[to, at_row : at_row + LAG] = paired[pl.ds(s, LAG, stride=BLOCK), :]
            if s % 2 == 0:
                last[to] = coded[s : s + 2]
        for dz in (4, 3, 5, 2, 6, 1, 7, 0):
            to = zs * n + lax.rem(z + dz, zs)
            for src, dst, send, recv in ((psend, p3, p3_send, p3_recv), (last, last_in, last_send, last_recv)):
                if turn == 0 and dz == 0:
                    pltpu.make_async_copy(src.at[to], dst.at[chip], recv.at[turn]).start()
                else:
                    for half in range(2 if src is psend else 1):
                        some = pl.ds(half * LAG, LAG) if src is psend else pl.ds(0, 2)
                        pltpu.make_async_remote_copy(
                            src_ref=src.at[to, some], dst_ref=dst.at[chip, some], send_sem=send, recv_sem=recv.at[turn],
                            device_id=(chan, to * 2 + core), device_id_type=MESH,
                        ).start()

    sums = [jnp.zeros((ROWS, LANE), f32)] * 2 + [jnp.zeros((2, LANE), f32)]
    for turn, n in enumerate(order):
        for ref, recv in ((p3, p3_recv), (last_in, last_recv)):
            arrived = ref.at[pl.ds(zs * n, zs)]
            pltpu.make_async_copy(arrived, arrived, recv.at[turn]).wait()
        for j in range(zs):
            piece = p3[zs * n + j]
            pair = last_in[zs * n + j]
            scales = scale_of((lax.bitwise_and(pair, 65535) - 32768).astype(f32))
            spread = jnp.concatenate([jnp.broadcast_to(scales[s : s + 1], (LAG, LANE)) for s in range(2)], axis=0)
            sums[0] += upper(piece) * spread
            sums[1] += upper(piece * 65536) * spread
            sums[2] += upper(pair) * scales
    final = 1.0 / (TOP * math.sqrt(n_tm * 2 * samples))
    for s in range(2):
        out_ref[s, 0:LAG] = sums[0][s * LAG : (s + 1) * LAG] * final
        out_ref[s, LAG : 2 * LAG] = sums[1][s * LAG : (s + 1) * LAG] * final
        out_ref[s, 2 * LAG : LAGS] = sums[2][s : s + 1] * final

    for copy in sent + halo_copies + half_copies:
        copy.wait_send()
    for ref, send in ((p3, p3_send), (last_in, last_send)):
        gone = ref.at[pl.ds(0, chips - 1)]
        pltpu.make_async_copy(gone, gone, send).wait()


def local(n_chan, n_tm, record, blocks, offsets):
    channels, width = record.shape
    groups = channels // BLOCK
    n_chunk = width // LANE
    per = n_chunk // NX
    chips = n_tm // 2
    dma = pltpu.SemaphoreType.DMA
    wide = (2 * n_chunk + 1) * LANE
    return pl.pallas_call(
        functools.partial(kernel, n_chan, n_tm),
        out_shape=pltpu.VMEM((2, LAGS, channels), f32),
        in_specs=[pl.BlockSpec(memory_space=pltpu.HBM)] * 3,
        out_specs=pl.BlockSpec(memory_space=pltpu.VMEM),
        scratch_shapes=[
            pltpu.SMEM((NBLK,), jnp.int32),
            pltpu.SMEM((2,), jnp.int32),
            pltpu.VMEM((groups, BLOCK, width), bf16),
            pltpu.VMEM((groups, BLOCK, width), bf16),
            pltpu.VMEM((2, groups, BLOCK, width), bf16),
            pltpu.VMEM((2, 2, BLOCK, LANE), bf16),
            pltpu.VMEM((groups + 1, BLOCK, LANE), bf16),
            pltpu.VMEM((2, groups + 1, BLOCK, LANE), bf16),
            pltpu.VMEM((2, NX, 2, per, BLOCK, LANE), bf16),
            pltpu.VMEM((4 * CUT, NX, per // CUT, BLOCK, LANE), bf16),
            pltpu.VMEM((2 * channels, wide), bf16),
            pltpu.VMEM((SHIFTS * BLOCK, wide), bf16),
            pltpu.VMEM((SHIFTS * BLOCK, LANE), f32),
            pltpu.VMEM((SHIFTS * BLOCK, LANE), f32),
            pltpu.VMEM((LAG * BLOCK, LANE), jnp.int32),
            pltpu.VMEM((chips, 2, LANE), jnp.int32),
            pltpu.VMEM((chips, 2, LANE), jnp.int32),
            pltpu.VMEM((chips, ROWS, LANE), jnp.int32),
            pltpu.VMEM((chips, ROWS, LANE), jnp.int32),
            dma((3,)), dma((2,)), dma((2,)), dma((2,)), dma((2,)), dma, dma((4 * CUT,)), dma, dma((4 * CUT,)),
            dma, dma((4 * CUT,)), dma, dma((2,)), dma, dma((2,)),
            *[pltpu.VMEM((NX, per // CUT, BLOCK, LANE), bf16)] * (4 * CUT),
            *[pltpu.VMEM((n_chan // NX, per // CUT, BLOCK, LANE), bf16)] * (4 * CUT),
        ],
        compiler_params=pltpu.CompilerParams(
            collective_id=0, has_side_effects=True, vmem_limit_bytes=(24 << 20)
        ),
        name="correlate",
    )(*[pltpu.with_memory_space_constraint(a, pltpu.HBM) for a in (blocks, offsets, record.reshape(groups, BLOCK, width))])


def solution(mesh):
    placed = (P("chan", "tm"), P(), P("tm"))
    run = functools.partial(local, mesh.shape["chan"], mesh.shape["tm"])
    return jax.shard_map(run, mesh=mesh, in_specs=placed, out_specs=P("tm", None, "chan"), check_vma=False)
```
